512 devices in a mesh: box: 64 (over y, x, core), samp: 8 (over z).
Axes of the slice: x: 4, y: 8, z: 8, core: 2. Of those that a mesh axis runs over, the one named last changes fastest.
Arguments:
- currents: bfloat16 [2, 1024, 24576], P(None, None, 'box'), may hold values from -6 to 6
- radiation: bfloat16 [2, 1024, 32, 64], P(None, None, None, 'samp'), may hold values from -0.125 to 0.125
- interp: float32 [7, 64], P(None, 'samp'), may hold values from -2 to 2
- anterp: float32 [7, 64], P(None, 'samp'), may hold values from -2 to 2
- weights: float32 [32], replicated, may hold values from 0.2 to 2
- operators: bfloat16 [2, 32, 64, 316], P(None, None, 'samp'), may hold values from -4 to 4
- pair_src: int32 [40960], P('box'), may hold values from 0 to 383
- pair_op: int32 [40960], P('box'), may hold values from 0 to 315
- pair_target: int32 [40960], P('box'), may hold values from 0 to 24575, as said below
Outputs:
- received: bfloat16 [2, 1024, 24576], P(None, 'samp', 'box')
The draws below stay inside these ranges and needn't reach their ends.
Inputs may be any that keep to these rules, and one draw needn't show every extreme that they name: The box group that owns pair i's target, pair_target[i] // 384, lies at most 2 groups from the pair's own group i // 640. At most 128 of one group's pairs name targets of any one other group, and the pairs of every group but the last name exactly 128 targets of the next group.
All inputs are finite; a program needn't handle non-finite values.
Results may differ from the reference program's by a relative error of at most 0.0058.
Values may be sent and summed in bfloat16 or wider, within the bound.
No kernel may reach another device: no remote copies, remote signals or barrier semaphores. Data moves between devices by JAX's collectives and lax.ppermute only.
A program may use at most 64 MiB of HBM per device.

```python
import math
import jax
import jax.numpy as jnp
from jax import lax

NT = 32
NP = 64
P_SIZE = 1024
NOPS = 316
WIDTH = 3
REACH = 2
BOX_DEV = 384
CAP = 128
PAIR_DEV = 640
BOXES = 24576
PAIRS = 40960


def draw_pair_target(key, part):
    key = jax.random.fold_in(key, 11)
    groups = PAIRS // PAIR_DEV
    key_load, key_keep, key_box, key_order = jax.random.split(key, 4)
    place = jnp.arange(PAIR_DEV, dtype=jnp.int32)
    offset = place // CAP - REACH
    owner = jnp.arange(groups, dtype=jnp.int32)[:, None]
    load = jax.random.randint(key_load, (groups, 1), 1, 5, dtype=jnp.int32)
    keep = jax.random.randint(key_keep, (groups, PAIR_DEV), 0, 4, dtype=jnp.int32) < load
    keep = jnp.logical_or(keep, offset[None, :] == 1)
    moved = jnp.where(keep, offset[None, :], 0)
    target = owner + moved
    inside = jnp.logical_and(target >= 0, target < groups)
    target = jnp.where(inside, target, owner)
    box_pick = jax.random.randint(key_box, (groups, PAIR_DEV), 0, BOX_DEV, dtype=jnp.int32)
    whole = target * BOX_DEV + box_pick
    scores = jax.random.randint(key_order, (groups, PAIR_DEV), 0, 1 << 20, dtype=jnp.int32) * PAIR_DEV + place[None, :]
    order = jnp.argsort(scores, axis=1)
    return jnp.take_along_axis(whole, order, axis=1).reshape(-1).astype(jnp.int32)


def place_ends(values, key, smallest, high):
    index_at = [jax.random.randint(jax.random.fold_in(key, axis), (), 0, length) for axis, length in enumerate(values.shape)]
    main_axis = values.shape.index(max(values.shape))
    next_to = index_at[:main_axis] + [(index_at[main_axis] + 1) % values.shape[main_axis]] + index_at[main_axis + 1:]
    return values.at[tuple(index_at)].set(smallest).at[tuple(next_to)].set(high)


def shard_levels(own_key, extent, cuts, least, top_value):
    def one(axis_at, blocks):
        steps = jax.random.uniform(jax.random.fold_in(jax.random.fold_in(own_key, 6), axis_at), (blocks,), jnp.float32, least / len(cuts), top_value / len(cuts))
        return jnp.repeat(jnp.exp(steps), extent[axis_at] // blocks).reshape((-1,) + (1,) * (len(extent) - axis_at - 1))

    level = one(*cuts[0])
    for cut in cuts[1:]:
        level = level * one(*cut)
    return level


def normal_values(key, extent, scale, most, pieces=(), kind=jnp.bfloat16):
    array = scale * jax.random.normal(key, extent, jnp.float32)
    if pieces:
        array = array * shard_levels(key, extent, pieces, -0.22, 0.18)
    return jnp.clip(array, -most, most).astype(kind)


def setup_inputs(seed: int = 0) -> dict:
    key_list = jax.random.split(jax.random.key(seed), 10)
    return {
        "currents": normal_values(key_list[0], (2, P_SIZE, BOXES), 1.0, 6.0, ((2, 64),)),
        "radiation": normal_values(key_list[1], (2, P_SIZE, NT, NP), (2 * P_SIZE) ** -0.5, 0.125, ((3, 8),)),
        "interp": normal_values(key_list[2], (2 * WIDTH + 1, NP), (2 * WIDTH + 1) ** -0.5, 2.0, ((1, 8),), jnp.float32),
        "anterp": normal_values(key_list[3], (2 * WIDTH + 1, NP), (2 * WIDTH + 1) ** -0.5, 2.0, ((1, 8),), jnp.float32),
        "weights": jnp.clip(jnp.exp(jax.random.uniform(key_list[4], (NT,), jnp.float32, math.log(0.2), math.log(2.0))), 0.2, 2.0),
        "operators": normal_values(key_list[5], (2, NT, NP, NOPS), 0.7, 4.0, ((2, 8),)),
        "pair_src": place_ends(jax.random.randint(key_list[6], (PAIRS,), 0, BOX_DEV), jax.random.fold_in(key_list[6], 1), 0, BOX_DEV - 1).astype(jnp.int32),
        "pair_op": place_ends(jax.random.randint(key_list[7], (PAIRS,), 0, NOPS), jax.random.fold_in(key_list[7], 1), 0, NOPS - 1).astype(jnp.int32),
        "pair_target": draw_pair_target(jax.random.fold_in(key_list[9], 71), 0),
    }


def along_phi(coeffs, values):
    total = jnp.zeros(values.shape, jnp.float32)
    for k in range(2 * WIDTH + 1):
        rolled = jnp.roll(values, -(k - WIDTH), axis=2)
        total = total + coeffs[k][None, None, :, None] * rolled
    return total


def reference(currents, radiation, interp, anterp, weights, operators, pair_src, pair_op, pair_target):
    count = NT * NP
    boxes = currents.shape[2]
    rad_re = radiation[0].reshape(P_SIZE, count)
    rad_im = radiation[1].reshape(P_SIZE, count)
    cur_re = currents[0]
    cur_im = currents[1]
    field_re = jnp.dot(rad_re.T, cur_re, preferred_element_type=jnp.float32) - jnp.dot(rad_im.T, cur_im, preferred_element_type=jnp.float32)
    field_im = jnp.dot(rad_re.T, cur_im, preferred_element_type=jnp.float32) + jnp.dot(rad_im.T, cur_re, preferred_element_type=jnp.float32)
    field = jnp.stack([field_re, field_im]).reshape(2, NT, NP, boxes)
    inter = along_phi(interp, field)
    groups = pair_src.shape[0] // PAIR_DEV

    def translate(group, incoming):
        group = jnp.asarray(group).astype(jnp.int32)
        start = (group * PAIR_DEV).astype(jnp.int32)
        source = lax.dynamic_slice_in_dim(pair_src, start, PAIR_DEV) + (group * BOX_DEV).astype(jnp.int32)
        opers = lax.dynamic_slice_in_dim(pair_op, start, PAIR_DEV)
        target = lax.dynamic_slice_in_dim(pair_target, start, PAIR_DEV)
        src_field = inter[:, :, :, source]
        oper_vals = operators[:, :, :, opers].astype(jnp.float32)
        part_re = oper_vals[0] * src_field[0] - oper_vals[1] * src_field[1]
        part_im = oper_vals[0] * src_field[1] + oper_vals[1] * src_field[0]
        contrib = jnp.stack([part_re, part_im]).astype(jnp.bfloat16)
        contrib = lax.optimization_barrier(contrib).astype(jnp.float32)
        return incoming.at[:, :, :, target].add(contrib)

    incoming = lax.fori_loop(0, groups, translate, jnp.zeros((2, NT, NP, boxes), jnp.float32))
    outgoing = along_phi(anterp, incoming) * weights[None, :, None, None]
    outgoing = outgoing.astype(jnp.bfloat16).reshape(2, count, boxes)
    recv_re = jnp.dot(rad_re, outgoing[0], preferred_element_type=jnp.float32) + jnp.dot(rad_im, outgoing[1], preferred_element_type=jnp.float32)
    recv_im = jnp.dot(rad_re, outgoing[1], preferred_element_type=jnp.float32) - jnp.dot(rad_im, outgoing[0], preferred_element_type=jnp.float32)
    return jnp.stack([recv_re, recv_im]).astype(jnp.bfloat16)
```

```python
import functools

import jax
import jax.numpy as jnp
from jax import lax
from jax.experimental import pallas as pl
from jax.experimental.pallas import tpu as pltpu
from jax.sharding import PartitionSpec as P

NT = 32
FD = 8
NS = NT * FD
EDGE = 3 * NT
P_SIZE = 1024
NOPS = 316
WIDTH = 3
BOX = 384
PAIR = 640
CAP = 128
STEPS = (1, -1, 2, -2)
SLOTS = CAP * len(STEPS)
BUF = 2 * NS + 16
RANKS = 8
BF = jnp.bfloat16
F32 = jnp.float32

NN = (((1,), (0,)), ((), ()))
NTR = (((1,), (1,)), ((), ()))
TN = (((0,), (0,)), ((), ()))


def dot(a, b, dims=NN):
    return lax.dot_general(a, b, dims, preferred_element_type=F32)


def iota(shape, dim):
    return lax.broadcasted_iota(jnp.int32, shape, dim)


def split(value):
    high = value.astype(BF)
    return high, (value - high.astype(F32)).astype(BF)


def local_place(shape, dim):
    at = iota(shape, dim)
    return at >> 3, at & 7


def edge_place(shape, dim):
    at = iota(shape, dim)
    return at & 31, at >> 5


def band(columns, diff, same):
    total = jnp.zeros(diff.shape, F32)
    for k in range(2 * WIDTH + 1):
        total = jnp.where(diff == k, columns[:, k : k + 1], total)
    return jnp.where(same, total, 0.0)


def one_hot(rows, index):
    return (iota((rows, index.shape[1]), 0) == index).astype(BF)


def field_kernel(rad, cur, field, low, high, total):
    step = pl.program_id(0)
    re, im = cur[0], cur[1]
    part = dot(rad[0], jnp.concatenate([re, im], axis=1))
    part = part + dot(rad[1], jnp.concatenate([-im, re], axis=1))

    @pl.when(step == 0)
    def _():
        total[...] = part

    @pl.when(step > 0)
    def _():
        total[...] = total[...] + part

    @pl.when(step == pl.num_programs(0) - 1)
    def _():
        whole = total[...]
        field[...] = whole
        rounded = whole.astype(BF)
        t_row, j_row = edge_place((EDGE, NS), 0)
        t_col, f_col = local_place((EDGE, NS), 1)
        same = t_row == t_col
        low[...] = dot(jnp.logical_and(same, f_col == j_row).astype(BF), rounded).astype(BF)
        high[...] = dot(jnp.logical_and(same, f_col == j_row + FD - WIDTH).astype(BF), rounded).astype(BF)


def prepare_kernel(
    field, interp_cols, anterp_cols, rad, digits, offset, oper, op_row,
    inter, halo_mat, src_pick, oper_slot, slot_ids, oper_own, q_up, q_down,
):
    shape = (NS, NS)
    t_row, g_row = local_place(shape, 0)
    t_col, f_col = local_place(shape, 1)
    mat_hi, mat_lo = split(band(interp_cols[...], f_col - g_row + WIDTH, t_row == t_col))
    f_hi, f_lo = split(field[...])
    inter[...] = dot(mat_hi, f_hi) + dot(mat_lo, f_hi) + dot(mat_hi, f_lo)
    shape = (NS, EDGE)
    t_row, g_row = local_place(shape, 0)
    t_col, j_col = edge_place(shape, 1)
    same = t_row == t_col
    below = split(band(interp_cols[...], j_col - g_row, same))
    above = split(band(interp_cols[...], j_col - g_row + FD + WIDTH, same))
    for part in range(2):
        halo_mat[part, 0] = below[part]
        halo_mat[part, 1] = above[part]

    step_of = offset[...]
    at = iota((8, PAIR), 0)
    cls = jnp.full((1, PAIR), -1, jnp.int32)
    for k, step in enumerate(STEPS):
        cls = jnp.where(step_of == step, k, cls)
    member = (at == cls).astype(BF)
    earlier = (iota((PAIR, PAIR), 0) < iota((PAIR, PAIR), 1)).astype(BF)
    before = dot(member, earlier) * member.astype(F32)
    rank = jnp.sum(before, axis=0, keepdims=True).astype(jnp.int32)
    slot = jnp.where(cls >= 0, cls * CAP + rank, -1)
    chosen = (iota((SLOTS, PAIR), 0) == slot).astype(BF)
    named = dot(digits[...], chosen, NTR)
    src = (16.0 * named[0:1] + named[1:2]).astype(jnp.int32)
    opn = (16.0 * named[2:3] + named[3:4]).astype(jnp.int32)
    filled = named[6:7] > 0.5
    src_pick[...] = one_hot(BOX, src)
    oper_slot[...] = dot(oper[...], one_hot(NOPS, opn)).astype(BF)
    oper_own[...] = dot(oper[...], one_hot(NOPS, op_row[...])).astype(BF)
    row = iota((16, SLOTS), 0)
    t_hi = jnp.where(filled, named[4:5], float(BOX // 16))
    t_lo = jnp.where(filled, named[5:6], 0.0)
    slot_ids[...] = jnp.where(row == 0, t_hi, jnp.where(row == 1, t_lo, 0.0)).astype(BF)

    shape = (NS, EDGE)
    t_row, f_row = local_place(shape, 0)
    t_col, j_col = edge_place(shape, 1)
    same = t_row == t_col
    up = split(band(anterp_cols[...], FD + j_col - f_row + WIDTH, same))
    down = split(band(anterp_cols[...], j_col - f_row, same))
    for c in range(2):
        cols = pl.ds(c * P_SIZE, P_SIZE)
        q_up[:, cols] = (dot(up[0], rad[c], TN) + dot(up[1], rad[c], TN)).astype(BF)
        q_down[:, cols] = (dot(down[0], rad[c], TN) + dot(down[1], rad[c], TN)).astype(BF)


def multiply(oper, re, im):
    o_re, o_im = oper[:NS, :].astype(F32), oper[NS:, :].astype(F32)
    return (o_re * re - o_im * im).astype(BF), (o_re * im + o_im * re).astype(BF)


def send_kernel(inter, halo_mat, below, above, src_pick, oper_slot, slot_ids, out0, out1, out2, out3, parts):
    whole = inter[...]
    for part in range(2):
        whole = whole + dot(halo_mat[part, 0], below[...]) + dot(halo_mat[part, 1], above[...])
    hi, lo = split(whole)
    parts[0] = hi
    parts[1] = lo
    pick = src_pick[...]
    re = dot(hi[:, :BOX], pick) + dot(lo[:, :BOX], pick)
    im = dot(hi[:, BOX:], pick) + dot(lo[:, BOX:], pick)
    c_re, c_im = multiply(oper_slot[...], re, im)
    for k, out in enumerate((out0, out1, out2, out3)):
        cols = slice(k * CAP, (k + 1) * CAP)
        out[0:NS, :] = c_re[:, cols]
        out[NS : 2 * NS, :] = c_im[:, cols]
        out[2 * NS :, :] = slot_ids[:, cols]


def own_kernel(parts, src_row, oper_own, target_row, own):
    pick = one_hot(BOX, src_row[...])
    hi, lo = parts[0], parts[1]
    re = dot(hi[:, :BOX], pick) + dot(lo[:, :BOX], pick)
    im = dot(hi[:, BOX:], pick) + dot(lo[:, BOX:], pick)
    c_re, c_im = multiply(oper_own[...], re, im)
    table = one_hot(BOX, target_row[...])
    own[:, :BOX] = dot(c_re, table, NTR)
    own[:, BOX:] = dot(c_im, table, NTR)


def matrix_kernel(rad, anterp_cols, q_below, q_above, out):
    shape = (NS, NS)
    t_row, f_row = local_place(shape, 0)
    t_col, g_col = local_place(shape, 1)
    mat_hi, mat_lo = split(band(anterp_cols[...], g_col - f_row + WIDTH, t_row == t_col))
    shape = (EDGE, NS)
    t_row, j_row = edge_place(shape, 0)
    t_col, g_col = local_place(shape, 1)
    same = t_row == t_col
    first = jnp.logical_and(same, g_col == j_row).astype(BF)
    last = jnp.logical_and(same, g_col == j_row + FD - WIDTH).astype(BF)
    for c in range(2):
        r = rad[c]
        cols = pl.ds(c * P_SIZE, P_SIZE)
        q = dot(r, mat_hi, TN) + dot(r, mat_lo, TN)
        q = q + dot(q_below[:, cols], first, TN) + dot(q_above[:, cols], last, TN)
        out[:, c * NS : (c + 1) * NS] = q.astype(BF)


def receive_kernel(own, matrix, got0, got1, got2, got3, out, stack):
    gots = (got0, got1, got2, got3)
    ids = jnp.concatenate([g[2 * NS :, :].astype(F32) for g in gots], axis=1)
    index = (16.0 * ids[0:1] + ids[1:2]).astype(jnp.int32)
    table = one_hot(BOX, index)
    re = own[:, :BOX] + dot(jnp.concatenate([g[0:NS, :] for g in gots], axis=1), table, NTR)
    im = own[:, BOX:] + dot(jnp.concatenate([g[NS : 2 * NS, :] for g in gots], axis=1), table, NTR)
    re, im = re.astype(BF), im.astype(BF)
    stack[0:NS, :BOX] = re
    stack[0:NS, BOX:] = im
    stack[NS:, :BOX] = im
    stack[NS:, BOX:] = -re

    @pl.loop(0, RANKS)
    def _(d):
        rows = pl.ds(pl.multiple_of(d * CAP, CAP), CAP)
        out[d] = dot(matrix[rows, :], stack[...]).astype(BF)


def sum_kernel(parts, out):
    total = parts[0].astype(F32)
    for d in range(1, RANKS):
        total = total + parts[d].astype(F32)
    out[0] = total[:, :BOX].astype(BF)
    out[1] = total[:, BOX:].astype(BF)


def call(kernel, outs, *args, scratch=(), flops=10**8, name=None, **kw):
    shapes = [jax.ShapeDtypeStruct(s, d) for s, d in outs]
    moved = sum(a.size * a.dtype.itemsize for a in args) + sum(s.size * s.dtype.itemsize for s in shapes)
    return pl.pallas_call(
        kernel,
        out_shape=shapes,
        scratch_shapes=list(scratch),
        compiler_params=pltpu.CompilerParams(vmem_limit_bytes=48 * 2**20),
        cost_estimate=pl.CostEstimate(flops=flops, bytes_accessed=moved, transcendentals=0),
        name=name,
        **kw,
    )(*args)


def around(value, axis, steps):
    count = lax.axis_size(axis)
    return lax.ppermute(value, axis, [(i, (i + steps) % count) for i in range(count)])


def along(value, axis, steps):
    count = lax.axis_size(axis)
    pairs = [(i, i + steps) for i in range(count) if 0 <= i + steps < count]
    return lax.ppermute(value, axis, pairs)


def digit_rows(values):
    return [values // 16, values % 16]


def on_device(
    currents, radiation, interp, anterp, weights, operators, pair_src, pair_op, pair_target
):
    rad = jnp.transpose(radiation, (0, 2, 3, 1)).reshape(2, NS, P_SIZE)
    oper = operators.reshape(2 * NS, NOPS)
    interp_cols = jnp.tile(interp.T, (NT, 1))
    anterp_cols = (weights[:, None, None] * anterp.T[None]).reshape(NS, 2 * WIDTH + 1)
    owner = pair_target // BOX
    target = pair_target - owner * BOX
    offset = owner - lax.axis_index("box")
    digits = jnp.stack(
        digit_rows(pair_src) + digit_rows(pair_op) + digit_rows(target)
        + [jnp.ones_like(target), jnp.zeros_like(target)]
    ).astype(BF)
    own_target = jnp.where(offset == 0, target, -1).reshape(1, PAIR)

    blocks = 4
    depth = P_SIZE // blocks
    whole = lambda r, c: pl.BlockSpec((r, c), lambda i: (0, 0))
    field, low, high = call(
        field_kernel,
        [((NS, 2 * BOX), F32), ((EDGE, 2 * BOX), BF), ((EDGE, 2 * BOX), BF)],
        rad, currents,
        scratch=[pltpu.VMEM((NS, 2 * BOX), F32)],
        flops=10**9,
        name="field",
        grid=(blocks,),
        in_specs=[
            pl.BlockSpec((2, NS, depth), lambda i: (0, 0, i)),
            pl.BlockSpec((2, depth, BOX), lambda i: (0, i, 0)),
        ],
        out_specs=[whole(NS, 2 * BOX), whole(EDGE, 2 * BOX), whole(EDGE, 2 * BOX)],
    )
    below = around(high, "samp", 1)
    above = around(low, "samp", -1)
    inter, halo_mat, src_pick, oper_slot, slot_ids, oper_own, q_up, q_down = call(
        prepare_kernel,
        [
            ((NS, 2 * BOX), F32), ((2, 2, NS, EDGE), BF), ((BOX, SLOTS), BF),
            ((2 * NS, SLOTS), BF), ((16, SLOTS), BF), ((2 * NS, PAIR), BF),
            ((EDGE, 2 * P_SIZE), BF), ((EDGE, 2 * P_SIZE), BF),
        ],
        field, interp_cols, anterp_cols, rad, digits, offset.reshape(1, PAIR), oper,
        pair_op.reshape(1, PAIR),
        flops=2 * 10**9,
        name="prepare",
    )
    *buffers, parts = call(
        send_kernel,
        [((BUF, CAP), BF)] * 4 + [((2, NS, 2 * BOX), BF)],
        inter, halo_mat, below, above, src_pick, oper_slot, slot_ids,
        name="send",
    )
    gots = [along(b, "box", step) for b, step in zip(buffers, STEPS)]
    q_up, q_down = lax.optimization_barrier((q_up, q_down, parts))[:2]
    q_below = around(q_up, "samp", 1)
    q_above = around(q_down, "samp", -1)
    (own,) = call(
        own_kernel,
        [((NS, 2 * BOX), F32)],
        parts, pair_src.reshape(1, PAIR), oper_own, own_target,
        flops=10**9,
        name="own",
    )
    (matrix,) = call(
        matrix_kernel,
        [((P_SIZE, 2 * NS), BF)],
        rad, anterp_cols, q_below, q_above,
        flops=10**9,
        name="matrix",
    )
    (terms,) = call(
        receive_kernel,
        [((RANKS, CAP, 2 * BOX), BF)],
        own, matrix, *gots,
        scratch=[pltpu.VMEM((2 * NS, 2 * BOX), BF)],
        flops=10**9,
        name="receive",
    )
    terms = lax.all_to_all(terms, "samp", 0, 0)
    (out,) = call(sum_kernel, [((2, P_SIZE // RANKS, BOX), BF)], terms, name="total")
    return out


def solution(mesh):
    return jax.shard_map(
        on_device,
        mesh=mesh,
        in_specs=(
            P(None, None, "box"),
            P(None, None, None, "samp"),
            P(None, "samp"),
            P(None, "samp"),
            P(),
            P(None, None, "samp", None),
            P("box"),
            P("box"),
            P("box"),
        ),
        out_specs=P(None, "samp", "box"),
        check_vma=False,
    )
```

```python
import functools

import jax
import jax.numpy as jnp
from jax import lax
from jax.experimental import pallas as pl
from jax.experimental.pallas import tpu as pltpu
from jax.sharding import PartitionSpec as P

NT = 32
FD = 8
NS = NT * FD
EDGE = 3 * NT
P_SIZE = 1024
NOPS = 316
WIDTH = 3
BOX = 384
PAIR = 640
CAP = 128
STEPS = (1, -1, 2, -2)
SLOTS = CAP * len(STEPS)
BUF = 2 * NS + 16
RANKS = 8
BF = jnp.bfloat16
SMEM = pl.BlockSpec(memory_space=pltpu.SMEM)
VMEM = pl.BlockSpec(memory_space=pltpu.VMEM)
F32 = jnp.float32

NN = (((1,), (0,)), ((), ()))
NTR = (((1,), (1,)), ((), ()))
TN = (((0,), (0,)), ((), ()))


def dot(a, b, dims=NN):
    return lax.dot_general(a, b, dims, preferred_element_type=F32)


def iota(shape, dim):
    return lax.broadcasted_iota(jnp.int32, shape, dim)


def split(value):
    high = value.astype(BF)
    return high, (value - high.astype(F32)).astype(BF)


def local_place(shape, dim):
    at = iota(shape, dim)
    return at >> 3, at & 7


def edge_place(shape, dim):
    at = iota(shape, dim)
    return at & 31, at >> 5


def band(columns, diff, same):
    total = jnp.zeros(diff.shape, F32)
    for k in range(2 * WIDTH + 1):
        total = jnp.where(diff == k, columns[:, k : k + 1], total)
    return jnp.where(same, total, 0.0)


def one_hot(rows, index):
    return (iota((rows, index.shape[1]), 0) == index).astype(BF)


def field_kernel(rad, cur, field, low, high, total):
    step = pl.program_id(0)
    re, im = cur[0], cur[1]
    part = dot(rad[0], jnp.concatenate([re, im], axis=1))
    part = part + dot(rad[1], jnp.concatenate([-im, re], axis=1))

    @pl.when(step == 0)
    def _():
        total[...] = part

    @pl.when(step > 0)
    def _():
        total[...] = total[...] + part

    @pl.when(step == pl.num_programs(0) - 1)
    def _():
        whole = total[...]
        field[...] = whole
        rounded = whole.astype(BF)
        t_row, j_row = edge_place((EDGE, NS), 0)
        t_col, f_col = local_place((EDGE, NS), 1)
        same = t_row == t_col
        low[...] = dot(jnp.logical_and(same, f_col == j_row).astype(BF), rounded).astype(BF)
        high[...] = dot(jnp.logical_and(same, f_col == j_row + FD - WIDTH).astype(BF), rounded).astype(BF)


def prepare_kernel(
    field, interp_cols, anterp_cols, rad, digits, offset, oper, op_row,
    inter, halo_mat, src_pick, oper_slot, slot_ids, oper_own, q_up, q_down,
):
    shape = (NS, NS)
    t_row, g_row = local_place(shape, 0)
    t_col, f_col = local_place(shape, 1)
    mat_hi, mat_lo = split(band(interp_cols[...], f_col - g_row + WIDTH, t_row == t_col))
    f_hi, f_lo = split(field[...])
    inter[...] = dot(mat_hi, f_hi) + dot(mat_lo, f_hi) + dot(mat_hi, f_lo)
    shape = (NS, EDGE)
    t_row, g_row = local_place(shape, 0)
    t_col, j_col = edge_place(shape, 1)
    same = t_row == t_col
    below = split(band(interp_cols[...], j_col - g_row, same))
    above = split(band(interp_cols[...], j_col - g_row + FD + WIDTH, same))
    for part in range(2):
        halo_mat[part, 0] = below[part]
        halo_mat[part, 1] = above[part]

    step_of = offset[...]
    at = iota((8, PAIR), 0)
    cls = jnp.full((1, PAIR), -1, jnp.int32)
    for k, step in enumerate(STEPS):
        cls = jnp.where(step_of == step, k, cls)
    member = (at == cls).astype(BF)
    earlier = (iota((PAIR, PAIR), 0) < iota((PAIR, PAIR), 1)).astype(BF)
    before = dot(member, earlier) * member.astype(F32)
    rank = jnp.sum(before, axis=0, keepdims=True).astype(jnp.int32)
    slot = jnp.where(cls >= 0, cls * CAP + rank, -1)
    chosen = (iota((SLOTS, PAIR), 0) == slot).astype(BF)
    named = dot(digits[...], chosen, NTR)
    src = (16.0 * named[0:1] + named[1:2]).astype(jnp.int32)
    opn = (16.0 * named[2:3] + named[3:4]).astype(jnp.int32)
    filled = named[6:7] > 0.5
    src_pick[...] = one_hot(BOX, src)
    oper_slot[...] = dot(oper[...], one_hot(NOPS, opn)).astype(BF)
    oper_own[...] = dot(oper[...], one_hot(NOPS, op_row[...])).astype(BF)
    row = iota((16, SLOTS), 0)
    t_hi = jnp.where(filled, named[4:5], float(BOX // 16))
    t_lo = jnp.where(filled, named[5:6], 0.0)
    slot_ids[...] = jnp.where(row == 0, t_hi, jnp.where(row == 1, t_lo, 0.0)).astype(BF)

    shape = (NS, EDGE)
    t_row, f_row = local_place(shape, 0)
    t_col, j_col = edge_place(shape, 1)
    same = t_row == t_col
    up = split(band(anterp_cols[...], FD + j_col - f_row + WIDTH, same))
    down = split(band(anterp_cols[...], j_col - f_row, same))
    for c in range(2):
        cols = pl.ds(c * P_SIZE, P_SIZE)
        q_up[:, cols] = (dot(up[0], rad[c], TN) + dot(up[1], rad[c], TN)).astype(BF)
        q_down[:, cols] = (dot(down[0], rad[c], TN) + dot(down[1], rad[c], TN)).astype(BF)


def multiply(oper, re, im):
    o_re, o_im = oper[:NS, :].astype(F32), oper[NS:, :].astype(F32)
    return (o_re * re - o_im * im).astype(BF), (o_re * im + o_im * re).astype(BF)


def send_kernel(inter, halo_mat, below, above, src_pick, oper_slot, slot_ids, out0, out1, out2, out3, parts):
    whole = inter[...]
    for part in range(2):
        whole = whole + dot(halo_mat[part, 0], below[...]) + dot(halo_mat[part, 1], above[...])
    hi, lo = split(whole)
    parts[0] = hi
    parts[1] = lo
    pick = src_pick[...]
    re = dot(hi[:, :BOX], pick) + dot(lo[:, :BOX], pick)
    im = dot(hi[:, BOX:], pick) + dot(lo[:, BOX:], pick)
    c_re, c_im = multiply(oper_slot[...], re, im)
    for k, out in enumerate((out0, out1, out2, out3)):
        cols = slice(k * CAP, (k + 1) * CAP)
        out[0:NS, :] = c_re[:, cols]
        out[NS : 2 * NS, :] = c_im[:, cols]
        out[2 * NS :, :] = slot_ids[:, cols]


def own_kernel(parts, src_row, oper_own, target_row, own):
    pick = one_hot(BOX, src_row[...])
    hi, lo = parts[0], parts[1]
    re = dot(hi[:, :BOX], pick) + dot(lo[:, :BOX], pick)
    im = dot(hi[:, BOX:], pick) + dot(lo[:, BOX:], pick)
    c_re, c_im = multiply(oper_own[...], re, im)
    table = one_hot(BOX, target_row[...])
    own[:, :BOX] = dot(c_re, table, NTR)
    own[:, BOX:] = dot(c_im, table, NTR)


def matrix_kernel(place, rad, anterp_cols, q_below, q_above, out):
    shape = (NS, NS)
    t_row, f_row = local_place(shape, 0)
    t_col, g_col = local_place(shape, 1)
    mat_hi, mat_lo = split(band(anterp_cols[...], g_col - f_row + WIDTH, t_row == t_col))
    shape = (EDGE, NS)
    t_row, j_row = edge_place(shape, 0)
    t_col, g_col = local_place(shape, 1)
    same = t_row == t_col
    first = jnp.logical_and(same, g_col == j_row).astype(BF)
    last = jnp.logical_and(same, g_col == j_row + FD - WIDTH).astype(BF)
    me = place[0]
    for c in range(2):
        r = rad[c]
        cols = pl.ds(c * P_SIZE, P_SIZE)
        q = dot(r, mat_hi, TN) + dot(r, mat_lo, TN)
        q = q + dot(q_below[:, cols], first, TN) + dot(q_above[:, cols], last, TN)
        q = q.astype(BF)
        for d in range(RANKS):
            rows = pl.ds(pl.multiple_of(((d - me) & (RANKS - 1)) * CAP, CAP), CAP)
            out[rows, c * NS : (c + 1) * NS] = q[d * CAP : (d + 1) * CAP]


def far_kernel(own, matrix, got0, got1, got2, got3, up3, far4, down3, stack):
    gots = (got0, got1, got2, got3)
    ids = jnp.concatenate([g[2 * NS :, :].astype(F32) for g in gots], axis=1)
    index = (16.0 * ids[0:1] + ids[1:2]).astype(jnp.int32)
    table = one_hot(BOX, index)
    re = own[:, :BOX] + dot(jnp.concatenate([g[0:NS, :] for g in gots], axis=1), table, NTR)
    im = own[:, BOX:] + dot(jnp.concatenate([g[NS : 2 * NS, :] for g in gots], axis=1), table, NTR)
    re, im = re.astype(BF), im.astype(BF)
    stack[0:NS, :BOX] = re
    stack[0:NS, BOX:] = im
    stack[NS:, :BOX] = im
    stack[NS:, BOX:] = -re
    for j, out in ((3, up3), (4, far4), (5, down3)):
        out[...] = dot(matrix[j * CAP : (j + 1) * CAP, :], stack[...]).astype(BF)


def near_kernel(matrix, stack, up1, down1, keep):
    for j, out in ((1, up1), (7, down1)):
        out[...] = dot(matrix[j * CAP : (j + 1) * CAP, :], stack[...]).astype(BF)
    for i, j in enumerate((0, 2, 6)):
        keep[i] = dot(matrix[j * CAP : (j + 1) * CAP, :], stack[...])


def relay_kernel(place, keep, from_up3, from_far4, from_down3, up2, down2):
    far = from_far4[...].astype(F32)
    even = place[1] == 0
    up2[...] = (keep[1] + from_up3[...].astype(F32) + jnp.where(even, far, 0.0)).astype(BF)
    down2[...] = (keep[2] + from_down3[...].astype(F32) + jnp.where(even, 0.0, far)).astype(BF)


def sum_kernel(keep, up1, down1, up2, down2, out):
    total = keep[0]
    for part in (up1, down1, up2, down2):
        total = total + part[...].astype(F32)
    out[0] = total[:, :BOX].astype(BF)
    out[1] = total[:, BOX:].astype(BF)


def call(kernel, outs, *args, scratch=(), flops=10**8, name=None, **kw):
    shapes = [jax.ShapeDtypeStruct(s, d) for s, d in outs]
    moved = sum(a.size * a.dtype.itemsize for a in args) + sum(s.size * s.dtype.itemsize for s in shapes)
    return pl.pallas_call(
        kernel,
        out_shape=shapes,
        scratch_shapes=list(scratch),
        compiler_params=pltpu.CompilerParams(vmem_limit_bytes=48 * 2**20),
        cost_estimate=pl.CostEstimate(flops=flops, bytes_accessed=moved, transcendentals=0),
        name=name,
        **kw,
    )(*args)


def around(value, axis, steps):
    count = lax.axis_size(axis)
    return lax.ppermute(value, axis, [(i, (i + steps) % count) for i in range(count)])


def outward(value, steps):
    groups, count = lax.axis_size("box"), lax.axis_size("samp")
    pairs = []
    for b in range(groups):
        for i in range(count):
            j = (i + (steps if b % 2 == 0 else -steps)) % count
            pairs.append((b * count + i, b * count + j))
    return lax.ppermute(value, ("box", "samp"), pairs)


def along(value, axis, steps):
    count = lax.axis_size(axis)
    pairs = [(i, i + steps) for i in range(count) if 0 <= i + steps < count]
    return lax.ppermute(value, axis, pairs)


def digit_rows(values):
    return [values // 16, values % 16]


def on_device(
    currents, radiation, interp, anterp, weights, operators, pair_src, pair_op, pair_target
):
    rad = jnp.transpose(radiation, (0, 2, 3, 1)).reshape(2, NS, P_SIZE)
    oper = operators.reshape(2 * NS, NOPS)
    interp_cols = jnp.tile(interp.T, (NT, 1))
    anterp_cols = (weights[:, None, None] * anterp.T[None]).reshape(NS, 2 * WIDTH + 1)
    owner = pair_target // BOX
    target = pair_target - owner * BOX
    offset = owner - lax.axis_index("box")
    digits = jnp.stack(
        digit_rows(pair_src) + digit_rows(pair_op) + digit_rows(target)
        + [jnp.ones_like(target), jnp.zeros_like(target)]
    ).astype(BF)
    own_target = jnp.where(offset == 0, target, -1).reshape(1, PAIR)

    blocks = 4
    depth = P_SIZE // blocks
    whole = lambda r, c: pl.BlockSpec((r, c), lambda i: (0, 0))
    field, low, high = call(
        field_kernel,
        [((NS, 2 * BOX), F32), ((EDGE, 2 * BOX), BF), ((EDGE, 2 * BOX), BF)],
        rad, currents,
        scratch=[pltpu.VMEM((NS, 2 * BOX), F32)],
        flops=10**9,
        name="field",
        grid=(blocks,),
        in_specs=[
            pl.BlockSpec((2, NS, depth), lambda i: (0, 0, i)),
            pl.BlockSpec((2, depth, BOX), lambda i: (0, i, 0)),
        ],
        out_specs=[whole(NS, 2 * BOX), whole(EDGE, 2 * BOX), whole(EDGE, 2 * BOX)],
    )
    below = around(high, "samp", 1)
    above = around(low, "samp", -1)
    inter, halo_mat, src_pick, oper_slot, slot_ids, oper_own, q_up, q_down = call(
        prepare_kernel,
        [
            ((NS, 2 * BOX), F32), ((2, 2, NS, EDGE), BF), ((BOX, SLOTS), BF),
            ((2 * NS, SLOTS), BF), ((16, SLOTS), BF), ((2 * NS, PAIR), BF),
            ((EDGE, 2 * P_SIZE), BF), ((EDGE, 2 * P_SIZE), BF),
        ],
        field, interp_cols, anterp_cols, rad, digits, offset.reshape(1, PAIR), oper,
        pair_op.reshape(1, PAIR),
        flops=2 * 10**9,
        name="prepare",
    )
    *buffers, parts = call(
        send_kernel,
        [((BUF, CAP), BF)] * 4 + [((2, NS, 2 * BOX), BF)],
        inter, halo_mat, below, above, src_pick, oper_slot, slot_ids,
        name="send",
    )
    gots = [along(b, "box", step) for b, step in zip(buffers, STEPS)]
    q_up, q_down = lax.optimization_barrier((q_up, q_down, parts))[:2]
    q_below = around(q_up, "samp", 1)
    q_above = around(q_down, "samp", -1)
    (own,) = call(
        own_kernel,
        [((NS, 2 * BOX), F32)],
        parts, pair_src.reshape(1, PAIR), oper_own, own_target,
        flops=10**9,
        name="own",
    )
    place = jnp.stack([lax.axis_index("samp"), lax.axis_index("box") % 2]).astype(jnp.int32)
    (matrix,) = call(
        matrix_kernel,
        [((P_SIZE, 2 * NS), BF)],
        place, rad, anterp_cols, q_below, q_above,
        flops=10**9,
        name="matrix",
        in_specs=[SMEM] + [VMEM] * 4,
    )
    block = (CAP, 2 * BOX)
    up3, far4, down3, stack = call(
        far_kernel,
        [(block, BF)] * 3 + [((2 * NS, 2 * BOX), BF)],
        own, matrix, *gots,
        flops=5 * 10**8,
        name="far",
    )
    from_up3 = around(up3, "samp", 1)
    from_far4 = outward(far4, 2)
    from_down3 = around(down3, "samp", -1)
    up1, down1, keep = call(
        near_kernel,
        [(block, BF)] * 2 + [((3,) + block, F32)],
        matrix, stack,
        flops=5 * 10**8,
        name="near",
    )
    from_up1 = around(up1, "samp", 1)
    from_down1 = around(down1, "samp", -1)
    up2, down2 = call(
        relay_kernel,
        [(block, BF)] * 2,
        place, keep, from_up3, from_far4, from_down3,
        name="relay",
        in_specs=[SMEM] + [VMEM] * 4,
    )
    from_up2 = around(up2, "samp", 2)
    from_down2 = around(down2, "samp", -2)
    (out,) = call(
        sum_kernel,
        [((2, P_SIZE // RANKS, BOX), BF)],
        keep, from_up1, from_down1, from_up2, from_down2,
        name="total",
    )
    return out


def solution(mesh):
    return jax.shard_map(
        on_device,
        mesh=mesh,
        in_specs=(
            P(None, None, "box"),
            P(None, None, None, "samp"),
            P(None, "samp"),
            P(None, "samp"),
            P(),
            P(None, None, "samp", None),
            P("box"),
            P("box"),
            P("box"),
        ),
        out_specs=P(None, "samp", "box"),
        check_vma=False,
    )
```

```python
import functools

import jax
import jax.numpy as jnp
from jax import lax
from jax.experimental import pallas as pl
from jax.experimental.pallas import tpu as pltpu
from jax.sharding import PartitionSpec as P

NT = 32
FD = 8
NS = NT * FD
EDGE = 3 * NT
P_SIZE = 1024
NOPS = 316
WIDTH = 3
REACH = 2
BOX = 384
PAIR = 640
CAP = 128
STEPS = (2, -2, 1, -1)
SLOTS = CAP * len(STEPS)
BUF = 2 * NS + 16
RANKS = 8
BF = jnp.bfloat16
SMEM = pl.BlockSpec(memory_space=pltpu.SMEM)
VMEM = pl.BlockSpec(memory_space=pltpu.VMEM)
HBM = pl.BlockSpec(memory_space=pltpu.HBM)
EDGE_PARTS = 4
F32 = jnp.float32

NN = (((1,), (0,)), ((), ()))
NTR = (((1,), (1,)), ((), ()))
TN = (((0,), (0,)), ((), ()))


def dot(a, b, dims=NN):
    return lax.dot_general(a, b, dims, preferred_element_type=F32)


def iota(shape, dim):
    return lax.broadcasted_iota(jnp.int32, shape, dim)


def split(value):
    high = value.astype(BF)
    return high, (value - high.astype(F32)).astype(BF)


def local_place(shape, dim):
    at = iota(shape, dim)
    return at >> 3, at & 7


def edge_place(shape, dim):
    at = iota(shape, dim)
    return at & 31, at >> 5


def band(columns, diff, same):
    total = jnp.zeros(diff.shape, F32)
    for k in range(2 * WIDTH + 1):
        total = jnp.where(diff == k, columns[:, k : k + 1], total)
    return jnp.where(same, total, 0.0)


def exact(a, b, dims=NN):
    return lax.dot_general(a, b, dims, precision=lax.Precision.HIGHEST, preferred_element_type=F32)


def own_columns(coeffs):
    _, f_row = local_place((NS, FD), 0)
    return exact((f_row == iota((NS, FD), 1)).astype(F32), coeffs, NTR)


def sample_weights(weights):
    t_row, _ = local_place((NS, NT), 0)
    same = t_row == iota((NS, NT), 1)
    return jnp.sum(jnp.where(same, weights, 0.0), axis=1, keepdims=True)


def one_hot(rows, index):
    return (iota((rows, index.shape[1]), 0) == index).astype(BF)


def edge_kernel(place, rad_all, anterp_all, weights_all, out, rad, anterp, weights, sems):
    parts = EDGE_PARTS
    depth = P_SIZE // parts
    copies = [
        pltpu.make_async_copy(anterp_all, anterp, sems.at[parts]),
        pltpu.make_async_copy(weights_all, weights, sems.at[parts + 1]),
    ]
    for i in range(parts):
        cols = pl.ds(i * depth, depth)
        copies.append(pltpu.make_async_copy(rad_all.at[:, cols], rad.at[:, cols], sems.at[i]))
    for copy in copies:
        copy.start()
    t_row, j_row = edge_place((EDGE, NS), 0)
    t_col, f_col = local_place((EDGE, NS), 1)
    first = jnp.where(place[1] == 0, FD - WIDTH, 0)
    pick = jnp.logical_and(t_row == t_col, f_col == j_row + first).astype(BF)
    t_lane, _ = edge_place((NT, CAP), 1)
    _, j_lane = edge_place((FD, CAP), 1)
    copies[0].wait()
    copies[1].wait()
    spread = exact(weights[...], (iota((NT, CAP), 0) == t_lane).astype(F32))
    coeffs = exact(anterp[...], (iota((FD, CAP), 0) == j_lane + first).astype(F32)) * spread
    high, low = split(jnp.concatenate([coeffs, jnp.zeros((1, CAP), F32)], axis=0))
    out[2 * EDGE :, :] = jnp.zeros((16, P_SIZE), BF)
    out[2 * EDGE :, 0:CAP] = jnp.concatenate([high.astype(F32), low.astype(F32)], axis=0).astype(BF)
    for i in range(parts):
        copies[2 + i].wait()
        cols = slice(i * depth, (i + 1) * depth)
        for c in range(2):
            out[c * EDGE : (c + 1) * EDGE, cols] = dot(pick, rad[c * NS : (c + 1) * NS, cols]).astype(BF)


def radiate(rad, cur, rows):
    with_re = dot(rad, cur[0])
    with_im = dot(rad, cur[1])
    return with_re[:rows] - with_im[rows:], with_im[:rows] + with_re[rows:]


def field_kernel(rad, cur, field):
    re, im = radiate(rad[...], cur, NS)
    field[:, :BOX] = re
    field[:, BOX:] = im


def prepare_kernel(
    place, field, interp, pair_src, pair_op, pair_target, oper,
    inter, halo_mat, src_pick, oper_slot, slot_ids, oper_own, own_rows,
):
    columns = own_columns(interp[...])
    shape = (NS, NS)
    t_row, g_row = local_place(shape, 0)
    t_col, f_col = local_place(shape, 1)
    mat_hi, mat_lo = split(band(columns, f_col - g_row + WIDTH, t_row == t_col))
    f_hi, f_lo = split(field[...])
    inter[...] = dot(mat_hi, f_hi) + dot(mat_lo, f_hi) + dot(mat_hi, f_lo)
    shape = (NS, EDGE)
    t_row, g_row = local_place(shape, 0)
    t_col, j_col = edge_place(shape, 1)
    for side in range(2):
        base = jnp.where(place[1] == side, 0, FD + WIDTH)
        mats = split(band(columns, j_col - g_row + base, t_row == t_col))
        for part in range(2):
            halo_mat[side, part] = mats[part]

    src_row, op_row = pair_src[...].reshape(1, PAIR), pair_op[...].reshape(1, PAIR)
    ahead = pair_target[...].reshape(1, PAIR) - place[2] * BOX
    step_of = jnp.full((1, PAIR), -REACH, jnp.int32)
    for k in range(1 - REACH, REACH + 1):
        step_of = step_of + (ahead >= k * BOX).astype(jnp.int32)
    target = ahead - step_of * BOX
    row = iota((8, PAIR), 0)
    own_rows[...] = jnp.where(row == 0, src_row, jnp.where(step_of == 0, target, -1))
    step_of = step_of * (2 * place[1] - 1)
    digits = jnp.ones((8, PAIR), jnp.int32)
    for k, value in enumerate((src_row, op_row, target)):
        digits = jnp.where(row == 2 * k, value >> 4, digits)
        digits = jnp.where(row == 2 * k + 1, value & 15, digits)
    digits = digits.astype(F32).astype(BF)

    at = iota((8, PAIR), 0)
    cls = jnp.full((1, PAIR), -1, jnp.int32)
    for k, step in enumerate(STEPS):
        cls = jnp.where(step_of == step, k, cls)
    member = (at == cls).astype(BF)
    earlier = (iota((PAIR, PAIR), 0) < iota((PAIR, PAIR), 1)).astype(BF)
    before = dot(member, earlier) * member.astype(F32)
    rank = jnp.sum(before, axis=0, keepdims=True).astype(jnp.int32)
    slot = jnp.where(cls >= 0, cls * CAP + rank, -1)
    chosen = (iota((SLOTS, PAIR), 0) == slot).astype(BF)
    named = dot(digits, chosen, NTR)
    src = (16.0 * named[0:1] + named[1:2]).astype(jnp.int32)
    opn = (16.0 * named[2:3] + named[3:4]).astype(jnp.int32)
    filled = named[6:7] > 0.5
    src_pick[...] = one_hot(BOX, src)
    oper_slot[...] = dot(oper[...], one_hot(NOPS, opn)).astype(BF)
    oper_own[...] = dot(oper[...], one_hot(NOPS, op_row)).astype(BF)
    row = iota((16, SLOTS), 0)
    t_hi = jnp.where(filled, named[4:5], float(BOX // 16))
    t_lo = jnp.where(filled, named[5:6], 0.0)
    slot_ids[...] = jnp.where(row == 0, t_hi, jnp.where(row == 1, t_lo, 0.0)).astype(BF)


def with_edge(inter, mats, edge, cur):
    re, im = radiate(edge[: 2 * EDGE, :], cur, EDGE)
    halo = jnp.concatenate([re, im], axis=1).astype(BF)
    return inter[...] + dot(mats[0], halo) + dot(mats[1], halo)


def first_edge_kernel(inter, halo_mat, edge, cur, out):
    out[...] = with_edge(inter, (halo_mat[0, 0], halo_mat[0, 1]), edge, cur)


def multiply(oper, re, im):
    o_re, o_im = oper[:NS, :].astype(F32), oper[NS:, :].astype(F32)
    return (o_re * re - o_im * im).astype(BF), (o_re * im + o_im * re).astype(BF)


def send_kernel(inter, halo_mat, edge, cur, src_pick, oper_slot, slot_ids, out0, out1, out2, out3, parts):
    whole = with_edge(inter, (halo_mat[1, 0], halo_mat[1, 1]), edge, cur)
    hi, lo = split(whole)
    parts[0] = hi
    parts[1] = lo
    pick = src_pick[...]
    re = dot(hi[:, :BOX], pick) + dot(lo[:, :BOX], pick)
    im = dot(hi[:, BOX:], pick) + dot(lo[:, BOX:], pick)
    c_re, c_im = multiply(oper_slot[...], re, im)
    for k, out in enumerate((out0, out1, out2, out3)):
        cols = slice(k * CAP, (k + 1) * CAP)
        out[0:NS, :] = c_re[:, cols]
        out[NS : 2 * NS, :] = c_im[:, cols]
        out[2 * NS :, :] = slot_ids[:, cols]


def own_kernel(parts, own_rows, oper_own, own):
    pick = one_hot(BOX, own_rows[0:1, :])
    hi, lo = parts[0], parts[1]
    re = dot(hi[:, :BOX], pick) + dot(lo[:, :BOX], pick)
    im = dot(hi[:, BOX:], pick) + dot(lo[:, BOX:], pick)
    c_re, c_im = multiply(oper_own[...], re, im)
    table = one_hot(BOX, own_rows[1:2, :])
    own[:, :BOX] = dot(c_re, table, NTR)
    own[:, BOX:] = dot(c_im, table, NTR)


def own_matrix_kernel(rad, anterp, weights, out):
    columns = own_columns(anterp[...]) * sample_weights(weights[...])
    shape = (NS, NS)
    t_row, f_row = local_place(shape, 0)
    t_col, g_col = local_place(shape, 1)
    mat_hi, mat_lo = split(band(columns, g_col - f_row + WIDTH, t_row == t_col))
    for c in range(2):
        r = rad[c * NS : (c + 1) * NS, :]
        out[:, c * NS : (c + 1) * NS] = dot(r, mat_hi, TN) + dot(r, mat_lo, TN)


def matrix_kernel(place, own, edge0, edge1, out):
    shape = (EDGE, NS)
    t_row, j_row = edge_place(shape, 0)
    t_col, g_col = local_place(shape, 1)
    mats = []
    for side, edge in enumerate((edge0, edge1)):
        tail = edge[2 * EDGE :, 0:CAP].astype(F32)
        cols = (tail[0:8] + tail[8:16]).T[:EDGE]
        base = jnp.where(place[1] == side, 2 * WIDTH, WIDTH - FD)
        mats.append(band(cols, g_col - j_row + base, t_row == t_col))
    high, low = split(jnp.concatenate(mats, axis=0))
    me = place[0]
    for c in range(2):
        rows = slice(c * EDGE, (c + 1) * EDGE)
        edges = jnp.concatenate([edge0[rows, :], edge1[rows, :]], axis=0)
        cols = slice(c * NS, (c + 1) * NS)
        q = (own[:, cols] + dot(edges, high, TN) + dot(edges, low, TN)).astype(BF)
        for d in range(RANKS):
            rows = pl.ds(pl.multiple_of(((d - me) & (RANKS - 1)) * CAP, CAP), CAP)
            out[rows, cols] = q[d * CAP : (d + 1) * CAP]


def far_kernel(own, matrix, got0, got1, got2, got3, up3, far4, down3, stack):
    gots = (got0, got1, got2, got3)
    ids = jnp.concatenate([g[2 * NS :, :].astype(F32) for g in gots], axis=1)
    index = (16.0 * ids[0:1] + ids[1:2]).astype(jnp.int32)
    table = one_hot(BOX, index)
    re = own[:, :BOX] + dot(jnp.concatenate([g[0:NS, :] for g in gots], axis=1), table, NTR)
    im = own[:, BOX:] + dot(jnp.concatenate([g[NS : 2 * NS, :] for g in gots], axis=1), table, NTR)
    re, im = re.astype(BF), im.astype(BF)
    stack[0:NS, :BOX] = re
    stack[0:NS, BOX:] = im
    stack[NS:, :BOX] = im
    stack[NS:, BOX:] = -re
    for j, out in ((3, up3), (4, far4), (5, down3)):
        out[...] = dot(matrix[j * CAP : (j + 1) * CAP, :], stack[...]).astype(BF)


def near_kernel(matrix, stack, up1, down1, keep):
    for j, out in ((1, up1), (7, down1)):
        out[...] = dot(matrix[j * CAP : (j + 1) * CAP, :], stack[...]).astype(BF)
    for i, j in enumerate((0, 2, 6)):
        keep[i] = dot(matrix[j * CAP : (j + 1) * CAP, :], stack[...])


def relay_kernel(place, keep, from_up3, from_far4, from_down3, up2, down2):
    far = from_far4[...].astype(F32)
    even = place[1] == 0
    up2[...] = (keep[1] + from_up3[...].astype(F32) + jnp.where(even, far, 0.0)).astype(BF)
    down2[...] = (keep[2] + from_down3[...].astype(F32) + jnp.where(even, 0.0, far)).astype(BF)


def sum_kernel(keep, up1, down1, up2, down2, out):
    total = keep[0]
    for part in (up1, down1, up2, down2):
        total = total + part[...].astype(F32)
    out[0] = total[:, :BOX].astype(BF)
    out[1] = total[:, BOX:].astype(BF)


def call(kernel, outs, *args, scratch=(), flops=10**8, name=None, vmem=24, **kw):
    shapes = [jax.ShapeDtypeStruct(s, d) for s, d in outs]
    moved = sum(a.size * a.dtype.itemsize for a in args) + sum(s.size * s.dtype.itemsize for s in shapes)
    return pl.pallas_call(
        kernel,
        out_shape=shapes,
        scratch_shapes=list(scratch),
        compiler_params=pltpu.CompilerParams(vmem_limit_bytes=vmem * 2**20),
        cost_estimate=pl.CostEstimate(flops=flops, bytes_accessed=moved, transcendentals=0),
        name=name,
        **kw,
    )(*args)


def around(value, axis, steps):
    count = lax.axis_size(axis)
    return lax.ppermute(value, axis, [(i, (i + steps) % count) for i in range(count)])


def outward(value, steps):
    groups, count = lax.axis_size("box"), lax.axis_size("samp")
    pairs = []
    for b in range(groups):
        for i in range(count):
            j = (i + (steps if b % 2 == 0 else -steps)) % count
            pairs.append((b * count + i, b * count + j))
    return lax.ppermute(value, ("box", "samp"), pairs)


def across(value):
    groups = lax.axis_size("box")
    return lax.ppermute(value, "box", [(b, b ^ 1) for b in range(groups)])


def sideways(value, steps):
    groups = lax.axis_size("box")
    pairs = [(b, b + steps * (1 if b % 2 else -1)) for b in range(groups)]
    return lax.ppermute(value, "box", [(b, to) for b, to in pairs if 0 <= to < groups])


def on_device(
    currents, radiation, interp, anterp, weights, operators, pair_src, pair_op, pair_target
):
    rad = jnp.transpose(radiation, (0, 2, 3, 1)).reshape(2 * NS, P_SIZE)
    oper = operators.reshape(2 * NS, NOPS)
    weights = weights.reshape(1, NT)
    group = lax.axis_index("box")
    place = jnp.stack([lax.axis_index("samp"), group % 2, group]).astype(jnp.int32)
    (edge,) = call(
        edge_kernel,
        [((2 * EDGE + 16, P_SIZE), BF)],
        place, rad, anterp, weights,
        scratch=[
            pltpu.VMEM((2 * NS, P_SIZE), BF),
            pltpu.VMEM((2 * WIDTH + 1, FD), F32),
            pltpu.VMEM((1, NT), F32),
            pltpu.SemaphoreType.DMA((EDGE_PARTS + 2,)),
        ],
        vmem=60,
        name="edge",
        in_specs=[SMEM] + [HBM] * 3,
    )
    edge0 = outward(edge, 1)

    (field,) = call(field_kernel, [((NS, 2 * BOX), F32)], rad, currents, flops=10**9, name="field")
    inter, halo_mat, src_pick, oper_slot, slot_ids, oper_own, own_rows = call(
        prepare_kernel,
        [
            ((NS, 2 * BOX), F32), ((2, 2, NS, EDGE), BF), ((BOX, SLOTS), BF),
            ((2 * NS, SLOTS), BF), ((16, SLOTS), BF), ((2 * NS, PAIR), BF), ((8, PAIR), jnp.int32),
        ],
        place, field, interp, pair_src, pair_op, pair_target, oper,
        flops=10**9,
        name="prepare",
        in_specs=[SMEM] + [VMEM] * 6,
    )
    (own_matrix,) = call(
        own_matrix_kernel, [((P_SIZE, 2 * NS), F32)], rad, anterp, weights, flops=10**9, name="own_matrix"
    )
    edge0, inter, own_matrix = lax.optimization_barrier((edge0, inter, own_matrix))
    edge1 = across(edge0)
    (inter,) = call(
        first_edge_kernel, [((NS, 2 * BOX), F32)], inter, halo_mat, edge0, currents,
        flops=4 * 10**8, name="first_edge",
    )
    *buffers, parts = call(
        send_kernel,
        [((BUF, CAP), BF)] * 4 + [((2, NS, 2 * BOX), BF)],
        inter, halo_mat, edge1, currents, src_pick, oper_slot, slot_ids,
        flops=4 * 10**8,
        name="send",
    )
    gots = [sideways(b, step) for b, step in zip(buffers, STEPS)]
    (own,) = call(
        own_kernel,
        [((NS, 2 * BOX), F32)],
        parts, own_rows, oper_own,
        flops=10**9,
        name="own",
    )
    (matrix,) = call(
        matrix_kernel,
        [((P_SIZE, 2 * NS), BF)],
        place, own_matrix, edge0, edge1,
        flops=10**9,
        name="matrix",
        in_specs=[SMEM] + [VMEM] * 3,
    )
    block = (CAP, 2 * BOX)
    up3, far4, down3, stack = call(
        far_kernel,
        [(block, BF)] * 3 + [((2 * NS, 2 * BOX), BF)],
        own, matrix, *gots,
        flops=5 * 10**8,
        name="far",
    )
    from_up3 = around(up3, "samp", 1)
    from_far4 = outward(far4, 2)
    from_down3 = around(down3, "samp", -1)
    up1, down1, keep = call(
        near_kernel,
        [(block, BF)] * 2 + [((3,) + block, F32)],
        matrix, stack,
        flops=5 * 10**8,
        name="near",
    )
    from_up1 = around(up1, "samp", 1)
    from_down1 = around(down1, "samp", -1)
    up2, down2 = call(
        relay_kernel,
        [(block, BF)] * 2,
        place, keep, from_up3, from_far4, from_down3,
        name="relay",
        in_specs=[SMEM] + [VMEM] * 4,
    )
    from_up2 = around(up2, "samp", 2)
    from_down2 = around(down2, "samp", -2)
    (out,) = call(
        sum_kernel,
        [((2, P_SIZE // RANKS, BOX), BF)],
        keep, from_up1, from_down1, from_up2, from_down2,
        name="total",
    )
    return out


def solution(mesh):
    return jax.shard_map(
        on_device,
        mesh=mesh,
        in_specs=(
            P(None, None, "box"),
            P(None, None, None, "samp"),
            P(None, "samp"),
            P(None, "samp"),
            P(),
            P(None, None, "samp", None),
            P("box"),
            P("box"),
            P("box"),
        ),
        out_specs=P(None, "samp", "box"),
        check_vma=False,
    )
```

```python
import functools

import jax
import jax.numpy as jnp
from jax import lax
from jax.experimental import pallas as pl
from jax.experimental.pallas import tpu as pltpu
from jax.sharding import PartitionSpec as P

NT = 32
FD = 8
NS = NT * FD
EDGE = 3 * NT
P_SIZE = 1024
NOPS = 316
WIDTH = 3
REACH = 2
BOX = 384
PAIR = 640
CAP = 128
STEPS = (2, -2, 1, -1)
SLOTS = CAP * len(STEPS)
BUF = 2 * NS + 16
RANKS = 8
OUTWARD = (1, 3, 6)
INWARD = (7, 4)
KEPT = (0, 2, 5)
BF = jnp.bfloat16
HBM = pl.BlockSpec(memory_space=pltpu.HBM)
EDGE_PARTS = 4
F32 = jnp.float32

NN = (((1,), (0,)), ((), ()))
NTR = (((1,), (1,)), ((), ()))
TN = (((0,), (0,)), ((), ()))


def dot(a, b, dims=NN):
    return lax.dot_general(a, b, dims, preferred_element_type=F32)


def iota(shape, dim):
    return lax.broadcasted_iota(jnp.int32, shape, dim)


def split(value):
    high = value.astype(BF)
    return high, (value - high.astype(F32)).astype(BF)


def local_place(shape, dim):
    at = iota(shape, dim)
    return at >> 3, at & 7


def edge_place(shape, dim):
    at = iota(shape, dim)
    return at & 31, at >> 5


def band(columns, diff, same):
    total = jnp.zeros(diff.shape, F32)
    for k in range(2 * WIDTH + 1):
        total = jnp.where(diff == k, columns[:, k : k + 1], total)
    return jnp.where(same, total, 0.0)


def exact(a, b, dims=NN):
    return lax.dot_general(a, b, dims, precision=lax.Precision.HIGHEST, preferred_element_type=F32)


def own_columns(coeffs):
    _, f_row = local_place((NS, FD), 0)
    return exact((f_row == iota((NS, FD), 1)).astype(F32), coeffs, NTR)


def sample_weights(weights):
    t_row, _ = local_place((NS, NT), 0)
    same = t_row == iota((NS, NT), 1)
    return jnp.sum(jnp.where(same, weights, 0.0), axis=1, keepdims=True)


def parity():
    return lax.rem(lax.axis_index("box"), 2)


def one_hot(rows, index):
    return (iota((rows, index.shape[1]), 0) == index).astype(BF)


def edge_kernel(rad_all, anterp_all, weights_all, out, rad, anterp, weights, sems):
    parts = EDGE_PARTS
    depth = P_SIZE // parts
    copies = [
        pltpu.make_async_copy(anterp_all, anterp, sems.at[parts]),
        pltpu.make_async_copy(weights_all, weights, sems.at[parts + 1]),
    ]
    for i in range(parts):
        cols = pl.ds(i * depth, depth)
        copies.append(pltpu.make_async_copy(rad_all.at[:, cols], rad.at[:, cols], sems.at[i]))
    for copy in copies:
        copy.start()
    t_row, j_row = edge_place((EDGE, NS), 0)
    t_col, f_col = local_place((EDGE, NS), 1)
    first = jnp.where(parity() == 0, FD - WIDTH, 0)
    pick = jnp.logical_and(t_row == t_col, f_col == j_row + first).astype(BF)
    for i in range(parts):
        copies[2 + i].wait()
        cols = slice(i * depth, (i + 1) * depth)
        for c in range(2):
            out[c * EDGE : (c + 1) * EDGE, cols] = dot(pick, rad[c * NS : (c + 1) * NS, cols]).astype(BF)
    t_lane, _ = edge_place((NT, CAP), 1)
    _, j_lane = edge_place((FD, CAP), 1)
    copies[0].wait()
    copies[1].wait()
    spread = exact(weights[...], (iota((NT, CAP), 0) == t_lane).astype(F32))
    coeffs = exact(anterp[...], (iota((FD, CAP), 0) == j_lane + first).astype(F32)) * spread
    high, low = split(jnp.concatenate([coeffs, jnp.zeros((1, CAP), F32)], axis=0))
    out[2 * EDGE :, 0:CAP] = jnp.concatenate([high.astype(F32), low.astype(F32)], axis=0).astype(BF)
    out[2 * EDGE :, CAP:] = jnp.zeros((16, P_SIZE - CAP), BF)


def radiate(rad, cur, rows):
    with_re = dot(rad, cur[0])
    with_im = dot(rad, cur[1])
    return with_re[:rows] - with_im[rows:], with_im[:rows] + with_re[rows:]


def field_kernel(rad, cur, field):
    re, im = radiate(rad[...], cur, NS)
    field[:, :BOX] = re
    field[:, BOX:] = im


def prepare_kernel(
    field, interp, pair_src, pair_op, pair_target, oper,
    inter, halo_mat, src_pick, oper_slot, slot_ids, oper_own, own_rows,
):
    columns = own_columns(interp[...])
    shape = (NS, NS)
    t_row, g_row = local_place(shape, 0)
    t_col, f_col = local_place(shape, 1)
    mat_hi, mat_lo = split(band(columns, f_col - g_row + WIDTH, t_row == t_col))
    f_hi, f_lo = split(field[...])
    inter[...] = dot(mat_hi, f_hi) + dot(mat_lo, f_hi) + dot(mat_hi, f_lo)
    shape = (NS, EDGE)
    t_row, g_row = local_place(shape, 0)
    t_col, j_col = edge_place(shape, 1)
    odd = parity()
    for side in range(2):
        base = jnp.where(odd == side, 0, FD + WIDTH)
        mats = split(band(columns, j_col - g_row + base, t_row == t_col))
        for part in range(2):
            halo_mat[side, part] = mats[part]

    src_row, op_row = pair_src[...].reshape(1, PAIR), pair_op[...].reshape(1, PAIR)
    ahead = pair_target[...].reshape(1, PAIR) - lax.axis_index("box") * BOX
    step_of = jnp.full((1, PAIR), -REACH, jnp.int32)
    for k in range(1 - REACH, REACH + 1):
        step_of = step_of + (ahead >= k * BOX).astype(jnp.int32)
    target = ahead - step_of * BOX
    row = iota((8, PAIR), 0)
    own_rows[...] = jnp.where(row == 0, src_row, jnp.where(step_of == 0, target, -1))
    step_of = step_of * (2 * odd - 1)
    digits = jnp.ones((8, PAIR), jnp.int32)
    for k, value in enumerate((src_row, op_row, target)):
        digits = jnp.where(row == 2 * k, value >> 4, digits)
        digits = jnp.where(row == 2 * k + 1, value & 15, digits)
    digits = digits.astype(F32).astype(BF)

    at = iota((8, PAIR), 0)
    cls = jnp.full((1, PAIR), -1, jnp.int32)
    for k, step in enumerate(STEPS):
        cls = jnp.where(step_of == step, k, cls)
    member = (at == cls).astype(BF)
    earlier = (iota((PAIR, PAIR), 0) < iota((PAIR, PAIR), 1)).astype(BF)
    before = dot(member, earlier) * member.astype(F32)
    rank = jnp.sum(before, axis=0, keepdims=True).astype(jnp.int32)
    slot = jnp.where(cls >= 0, cls * CAP + rank, -1)
    chosen = (iota((SLOTS, PAIR), 0) == slot).astype(BF)
    named = dot(digits, chosen, NTR)
    src = (16.0 * named[0:1] + named[1:2]).astype(jnp.int32)
    opn = (16.0 * named[2:3] + named[3:4]).astype(jnp.int32)
    filled = named[6:7] > 0.5
    src_pick[...] = one_hot(BOX, src)
    oper_slot[...] = dot(oper[...], one_hot(NOPS, opn)).astype(BF)
    oper_own[...] = dot(oper[...], one_hot(NOPS, op_row)).astype(BF)
    row = iota((16, SLOTS), 0)
    t_hi = jnp.where(filled, named[4:5], float(BOX // 16))
    t_lo = jnp.where(filled, named[5:6], 0.0)
    slot_ids[...] = jnp.where(row == 0, t_hi, jnp.where(row == 1, t_lo, 0.0)).astype(BF)


def with_edge(inter, mats, edge, cur):
    re, im = radiate(edge[: 2 * EDGE, :], cur, EDGE)
    halo = jnp.concatenate([re, im], axis=1).astype(BF)
    return inter[...] + dot(mats[0], halo) + dot(mats[1], halo)


def first_edge_kernel(inter, halo_mat, edge, cur, out):
    out[...] = with_edge(inter, (halo_mat[0, 0], halo_mat[0, 1]), edge, cur)


def multiply(oper, re, im):
    o_re, o_im = oper[:NS, :].astype(F32), oper[NS:, :].astype(F32)
    return (o_re * re - o_im * im).astype(BF), (o_re * im + o_im * re).astype(BF)


def send_kernel(inter, halo_mat, edge, cur, src_pick, oper_slot, slot_ids, out0, out1, out2, out3, parts):
    whole = with_edge(inter, (halo_mat[1, 0], halo_mat[1, 1]), edge, cur)
    hi, lo = split(whole)
    parts[0] = hi
    parts[1] = lo
    pick = src_pick[...]
    re = dot(hi[:, :BOX], pick) + dot(lo[:, :BOX], pick)
    im = dot(hi[:, BOX:], pick) + dot(lo[:, BOX:], pick)
    c_re, c_im = multiply(oper_slot[...], re, im)
    for k, out in enumerate((out0, out1, out2, out3)):
        cols = slice(k * CAP, (k + 1) * CAP)
        out[0:NS, :] = c_re[:, cols]
        out[NS : 2 * NS, :] = c_im[:, cols]
        out[2 * NS :, :] = slot_ids[:, cols]


def own_kernel(parts, own_rows, oper_own, own):
    pick = one_hot(BOX, own_rows[0:1, :])
    hi, lo = parts[0], parts[1]
    re = dot(hi[:, :BOX], pick) + dot(lo[:, :BOX], pick)
    im = dot(hi[:, BOX:], pick) + dot(lo[:, BOX:], pick)
    c_re, c_im = multiply(oper_own[...], re, im)
    table = one_hot(BOX, own_rows[1:2, :])
    own[:, :BOX] = dot(c_re, table, NTR)
    own[:, BOX:] = dot(c_im, table, NTR)


def matrix_rows(rad, edge0, edge1, mats, steps, out):
    me = lax.axis_index("samp")
    side = 1 - 2 * parity()
    for c in range(2):
        blocks = []
        for j in steps:
            cols = pl.ds(pl.multiple_of(((me + side * j) & (RANKS - 1)) * CAP, CAP), CAP)
            mine = rad[c * NS : (c + 1) * NS, cols]
            rows = slice(c * EDGE, (c + 1) * EDGE)
            blocks.append(jnp.concatenate([mine, edge0[rows, cols], edge1[rows, cols]], axis=0))
        both = dot(jnp.concatenate(blocks, axis=1), mats[...], TN)
        out[:, c * NS : (c + 1) * NS] = (both[:, :NS] + both[:, NS:]).astype(BF)


def matrix_kernel(rad, edge0, edge1, anterp, weights, mats, out):
    shape = (NS, NS)
    t_row, f_row = local_place(shape, 0)
    t_col, g_col = local_place(shape, 1)
    columns = own_columns(anterp[...]) * sample_weights(weights[...])
    bands = [band(columns, g_col - f_row + WIDTH, t_row == t_col)]
    shape = (EDGE, NS)
    t_row, j_row = edge_place(shape, 0)
    t_col, g_col = local_place(shape, 1)
    odd = parity()
    for side, edge in enumerate((edge0, edge1)):
        tail = edge[2 * EDGE :, 0:CAP].astype(F32)
        cols = (tail[0:8] + tail[8:16]).T[:EDGE]
        base = jnp.where(odd == side, 2 * WIDTH, WIDTH - FD)
        bands.append(band(cols, g_col - j_row + base, t_row == t_col))
    high, low = split(jnp.concatenate(bands, axis=0))
    mats[:, :NS] = high
    mats[:, NS:] = low
    matrix_rows(rad, edge0, edge1, mats, OUTWARD, out)


def far_kernel(own, matrix, got0, got1, got2, got3, out, stack):
    gots = (got0, got1, got2, got3)
    ids = jnp.concatenate([g[2 * NS :, :].astype(F32) for g in gots], axis=1)
    index = (16.0 * ids[0:1] + ids[1:2]).astype(jnp.int32)
    table = one_hot(BOX, index)
    re = own[:, :BOX] + dot(jnp.concatenate([g[0:NS, :] for g in gots], axis=1), table, NTR)
    im = own[:, BOX:] + dot(jnp.concatenate([g[NS : 2 * NS, :] for g in gots], axis=1), table, NTR)
    re, im = re.astype(BF), im.astype(BF)
    stack[0:NS, :BOX] = re
    stack[0:NS, BOX:] = im
    stack[NS:, :BOX] = im
    stack[NS:, BOX:] = -re
    out[...] = dot(matrix[...], stack[...]).astype(BF)


def near_kernel(rad, edge0, edge1, mats, stack, inward, keep, matrix):
    matrix_rows(rad, edge0, edge1, mats, INWARD + KEPT, matrix)
    cut = len(INWARD) * CAP
    inward[...] = dot(matrix[0:cut, :], stack[...]).astype(BF)
    keep[...] = dot(matrix[cut:, :], stack[...])


def relay_out_kernel(keep, from_inner, out2):
    out2[...] = (keep[CAP : 2 * CAP, :] + from_inner[CAP : 2 * CAP, :].astype(F32)).astype(BF)


def relay_in_kernel(keep, from_inner, from_outer, in3):
    far = from_inner[2 * CAP :, :].astype(F32) + from_outer[CAP:, :].astype(F32)
    in3[...] = (keep[2 * CAP :, :] + far).astype(BF)


def sum_kernel(keep, from_inner, from_outer, out2, in3, out):
    total = keep[0:CAP, :]
    for part in (from_inner[0:CAP, :], from_outer[0:CAP, :], out2[...], in3[...]):
        total = total + part.astype(F32)
    out[0] = total[:, :BOX].astype(BF)
    out[1] = total[:, BOX:].astype(BF)


def call(kernel, outs, *args, scratch=(), flops=10**8, name=None, vmem=24, **kw):
    shapes = [jax.ShapeDtypeStruct(s, d) for s, d in outs]
    moved = sum(a.size * a.dtype.itemsize for a in args) + sum(s.size * s.dtype.itemsize for s in shapes)
    return pl.pallas_call(
        kernel,
        out_shape=shapes,
        scratch_shapes=list(scratch),
        compiler_params=pltpu.CompilerParams(vmem_limit_bytes=vmem * 2**20),
        cost_estimate=pl.CostEstimate(flops=flops, bytes_accessed=moved, transcendentals=0),
        name=name,
        **kw,
    )(*args)


def outward(value, steps):
    groups, count = lax.axis_size("box"), lax.axis_size("samp")
    pairs = []
    for b in range(groups):
        for i in range(count):
            j = (i + (steps if b % 2 == 0 else -steps)) % count
            pairs.append((b * count + i, b * count + j))
    return lax.ppermute(value, ("box", "samp"), pairs)


def across(value):
    groups = lax.axis_size("box")
    return lax.ppermute(value, "box", [(b, b ^ 1) for b in range(groups)])


def sideways(value, steps):
    groups = lax.axis_size("box")
    pairs = [(b, b + steps * (1 if b % 2 else -1)) for b in range(groups)]
    return lax.ppermute(value, "box", [(b, to) for b, to in pairs if 0 <= to < groups])


def on_device(
    currents, radiation, interp, anterp, weights, operators, pair_src, pair_op, pair_target
):
    rad = jnp.transpose(radiation, (0, 2, 3, 1)).reshape(2 * NS, P_SIZE)
    oper = operators.reshape(2 * NS, NOPS)
    weights = weights.reshape(1, NT)
    (edge,) = call(
        edge_kernel,
        [((2 * EDGE + 16, P_SIZE), BF)],
        rad, anterp, weights,
        scratch=[
            pltpu.VMEM((2 * NS, P_SIZE), BF),
            pltpu.VMEM((2 * WIDTH + 1, FD), F32),
            pltpu.VMEM((1, NT), F32),
            pltpu.SemaphoreType.DMA((EDGE_PARTS + 2,)),
        ],
        vmem=58,
        name="edge",
        in_specs=[HBM] * 3,
    )
    edge0 = outward(edge, 1)

    (field,) = call(field_kernel, [((NS, 2 * BOX), F32)], rad, currents, flops=10**9, name="field")
    inter, halo_mat, src_pick, oper_slot, slot_ids, oper_own, own_rows = call(
        prepare_kernel,
        [
            ((NS, 2 * BOX), F32), ((2, 2, NS, EDGE), BF), ((BOX, SLOTS), BF),
            ((2 * NS, SLOTS), BF), ((16, SLOTS), BF), ((2 * NS, PAIR), BF), ((8, PAIR), jnp.int32),
        ],
        field, interp, pair_src, pair_op, pair_target, oper,
        flops=10**9,
        name="prepare",
    )
    edge0, inter = lax.optimization_barrier((edge0, inter))
    edge1 = across(edge0)
    (inter,) = call(
        first_edge_kernel, [((NS, 2 * BOX), F32)], inter, halo_mat, edge0, currents,
        flops=4 * 10**8, name="first_edge",
    )
    *buffers, parts = call(
        send_kernel,
        [((BUF, CAP), BF)] * 4 + [((2, NS, 2 * BOX), BF)],
        inter, halo_mat, edge1, currents, src_pick, oper_slot, slot_ids,
        flops=4 * 10**8,
        name="send",
    )
    gots = [sideways(b, step) for b, step in zip(buffers, STEPS)]
    (own,) = call(
        own_kernel,
        [((NS, 2 * BOX), F32)],
        parts, own_rows, oper_own,
        flops=10**9,
        name="own",
    )
    mats, matrix = call(
        matrix_kernel,
        [((NS + 2 * EDGE, 2 * NS), BF), ((len(OUTWARD) * CAP, 2 * NS), BF)],
        rad, edge0, edge1, anterp, weights,
        flops=10**9,
        name="matrix",
    )
    blocks = lambda steps: (steps * CAP, 2 * BOX)
    leaving, stack = call(
        far_kernel,
        [(blocks(len(OUTWARD)), BF), ((2 * NS, 2 * BOX), BF)],
        own, matrix, *gots,
        flops=5 * 10**8,
        name="far",
    )
    from_inner = outward(leaving, 1)
    inward, keep = call(
        near_kernel,
        [(blocks(len(INWARD)), BF), (blocks(len(KEPT)), F32)],
        rad, edge0, edge1, mats, stack,
        scratch=[pltpu.VMEM(((len(INWARD) + len(KEPT)) * CAP, 2 * NS), BF)],
        flops=10**9,
        name="near",
    )
    from_outer = outward(inward, -1)
    (out2,) = call(relay_out_kernel, [(blocks(1), BF)], keep, from_inner, name="relay_out")
    from_inner2 = outward(out2, 2)
    (in3,) = call(relay_in_kernel, [(blocks(1), BF)], keep, from_inner, from_outer, name="relay_in")
    from_outer3 = outward(in3, -3)
    (out,) = call(
        sum_kernel,
        [((2, P_SIZE // RANKS, BOX), BF)],
        keep, from_inner, from_outer, from_inner2, from_outer3,
        name="total",
    )
    return out


def solution(mesh):
    return jax.shard_map(
        on_device,
        mesh=mesh,
        in_specs=(
            P(None, None, "box"),
            P(None, None, None, "samp"),
            P(None, "samp"),
            P(None, "samp"),
            P(),
            P(None, None, "samp", None),
            P("box"),
            P("box"),
            P("box"),
        ),
        out_specs=P(None, "samp", "box"),
        check_vma=False,
    )
```

```python
import functools

import jax
import jax.numpy as jnp
from jax import lax
from jax.experimental import pallas as pl
from jax.experimental.pallas import tpu as pltpu
from jax.sharding import PartitionSpec as P

NT = 32
FD = 8
NS = NT * FD
EDGE = 3 * NT
P_SIZE = 1024
NOPS = 316
WIDTH = 3
REACH = 2
BOX = 384
PAIR = 640
CAP = 128
STEPS = (2, -2, 1, -1)
SLOTS = CAP * len(STEPS)
BUF = 2 * NS + 16
RANKS = 8
TAIL = RANKS * 2 * EDGE
OUTWARD = (1, 3, 6)
INWARD = (7, 4)
KEPT = (0, 2, 5)
BF = jnp.bfloat16
HBM = pl.BlockSpec(memory_space=pltpu.HBM)
EDGE_PARTS = 4
F32 = jnp.float32

NN = (((1,), (0,)), ((), ()))
NTR = (((1,), (1,)), ((), ()))
TN = (((0,), (0,)), ((), ()))


def dot(a, b, dims=NN):
    return lax.dot_general(a, b, dims, preferred_element_type=F32)


def iota(shape, dim):
    return lax.broadcasted_iota(jnp.int32, shape, dim)


def split(value):
    high = value.astype(BF)
    return high, (value - high.astype(F32)).astype(BF)


def local_place(shape, dim):
    at = iota(shape, dim)
    return at >> 3, at & 7


def edge_place(shape, dim):
    at = iota(shape, dim)
    return at & 31, at >> 5


def band(columns, diff, same):
    total = jnp.zeros(diff.shape, F32)
    for k in range(2 * WIDTH + 1):
        total = jnp.where(diff == k, columns[:, k : k + 1], total)
    return jnp.where(same, total, 0.0)


def exact(a, b, dims=NN):
    return lax.dot_general(a, b, dims, precision=lax.Precision.HIGHEST, preferred_element_type=F32)


def own_columns(coeffs):
    _, f_row = local_place((NS, FD), 0)
    return exact((f_row == iota((NS, FD), 1)).astype(F32), coeffs, NTR)


def sample_weights(weights):
    t_row, _ = local_place((NS, NT), 0)
    same = t_row == iota((NS, NT), 1)
    return jnp.sum(jnp.where(same, weights, 0.0), axis=1, keepdims=True)


def parity():
    return lax.rem(lax.axis_index("box"), 2)


def one_hot(rows, index):
    return (iota((rows, index.shape[1]), 0) == index).astype(BF)


def edge_kernel(rad_all, anterp_all, weights_all, out, rad, anterp, weights, sems):
    parts = EDGE_PARTS
    depth = P_SIZE // parts
    copies = [
        pltpu.make_async_copy(anterp_all, anterp, sems.at[parts]),
        pltpu.make_async_copy(weights_all, weights, sems.at[parts + 1]),
    ]
    for i in range(parts):
        cols = pl.ds(i * depth, depth)
        copies.append(pltpu.make_async_copy(rad_all.at[:, cols], rad.at[:, cols], sems.at[i]))
    for copy in copies:
        copy.start()
    t_row, j_row = edge_place((EDGE, NS), 0)
    t_col, f_col = local_place((EDGE, NS), 1)
    first = jnp.where(parity() == 0, FD - WIDTH, 0)
    pick = jnp.logical_and(t_row == t_col, f_col == j_row + first).astype(BF)
    for i in range(parts):
        copies[2 + i].wait()
        cols = slice(i * depth, (i + 1) * depth)
        for c in range(2):
            picked = dot(pick, rad[c * NS : (c + 1) * NS, cols]).astype(BF)
            for k in range(depth // CAP):
                row = (i * (depth // CAP) + k) * 2 * EDGE + c * EDGE
                out[row : row + EDGE, :] = picked[:, k * CAP : (k + 1) * CAP]
    t_lane, _ = edge_place((NT, CAP), 1)
    _, j_lane = edge_place((FD, CAP), 1)
    copies[0].wait()
    copies[1].wait()
    spread = exact(weights[...], (iota((NT, CAP), 0) == t_lane).astype(F32))
    coeffs = exact(anterp[...], (iota((FD, CAP), 0) == j_lane + first).astype(F32)) * spread
    high, low = split(jnp.concatenate([coeffs, jnp.zeros((1, CAP), F32)], axis=0))
    out[TAIL:, :] = jnp.concatenate([high.astype(F32), low.astype(F32)], axis=0).astype(BF)


def radiate(rad, cur, rows):
    with_re = dot(rad, cur[0])
    with_im = dot(rad, cur[1])
    return with_re[:rows] - with_im[rows:], with_im[:rows] + with_re[rows:]


def field_kernel(rad, cur, field):
    re, im = radiate(rad[...], cur, NS)
    field[:, :BOX] = re
    field[:, BOX:] = im


def prepare_kernel(
    field, interp, anterp, weights, pair_src, pair_op, pair_target, oper,
    inter, halo_mat, src_pick, oper_slot, slot_ids, oper_own, own_rows, own_mat,
):
    columns = own_columns(interp[...])
    shape = (NS, NS)
    t_row, g_row = local_place(shape, 0)
    t_col, f_col = local_place(shape, 1)
    mat_hi, mat_lo = split(band(columns, f_col - g_row + WIDTH, t_row == t_col))
    f_hi, f_lo = split(field[...])
    inter[...] = dot(mat_hi, f_hi) + dot(mat_lo, f_hi) + dot(mat_hi, f_lo)
    shape = (NS, EDGE)
    t_row, g_row = local_place(shape, 0)
    t_col, j_col = edge_place(shape, 1)
    odd = parity()
    for side in range(2):
        base = jnp.where(odd == side, 0, FD + WIDTH)
        mats = split(band(columns, j_col - g_row + base, t_row == t_col))
        for part in range(2):
            halo_mat[side, part] = mats[part]

    shape = (NS, NS)
    t_row, f_row = local_place(shape, 0)
    t_col, g_col = local_place(shape, 1)
    columns = own_columns(anterp[...]) * sample_weights(weights[...])
    own_mat[:, :NS], own_mat[:, NS:] = split(band(columns, g_col - f_row + WIDTH, t_row == t_col))

    src_row, op_row = pair_src[...].reshape(1, PAIR), pair_op[...].reshape(1, PAIR)
    ahead = pair_target[...].reshape(1, PAIR) - lax.axis_index("box") * BOX
    step_of = jnp.full((1, PAIR), -REACH, jnp.int32)
    for k in range(1 - REACH, REACH + 1):
        step_of = step_of + (ahead >= k * BOX).astype(jnp.int32)
    target = ahead - step_of * BOX
    row = iota((8, PAIR), 0)
    own_rows[...] = jnp.where(row == 0, src_row, jnp.where(step_of == 0, target, -1))
    step_of = step_of * (2 * odd - 1)
    digits = jnp.ones((8, PAIR), jnp.int32)
    for k, value in enumerate((src_row, op_row, target)):
        digits = jnp.where(row == 2 * k, value >> 4, digits)
        digits = jnp.where(row == 2 * k + 1, value & 15, digits)
    digits = digits.astype(F32).astype(BF)

    at = iota((8, PAIR), 0)
    cls = jnp.full((1, PAIR), -1, jnp.int32)
    for k, step in enumerate(STEPS):
        cls = jnp.where(step_of == step, k, cls)
    member = (at == cls).astype(BF)
    earlier = (iota((PAIR, PAIR), 0) < iota((PAIR, PAIR), 1)).astype(BF)
    before = dot(member, earlier) * member.astype(F32)
    rank = jnp.sum(before, axis=0, keepdims=True).astype(jnp.int32)
    slot = jnp.where(cls >= 0, cls * CAP + rank, -1)
    chosen = (iota((SLOTS, PAIR), 0) == slot).astype(BF)
    named = dot(digits, chosen, NTR)
    src = (16.0 * named[0:1] + named[1:2]).astype(jnp.int32)
    opn = (16.0 * named[2:3] + named[3:4]).astype(jnp.int32)
    filled = named[6:7] > 0.5
    src_pick[...] = one_hot(BOX, src)
    oper_slot[...] = dot(oper[...], one_hot(NOPS, opn)).astype(BF)
    oper_own[...] = dot(oper[...], one_hot(NOPS, op_row)).astype(BF)
    row = iota((16, SLOTS), 0)
    t_hi = jnp.where(filled, named[4:5], float(BOX // 16))
    t_lo = jnp.where(filled, named[5:6], 0.0)
    slot_ids[...] = jnp.where(row == 0, t_hi, jnp.where(row == 1, t_lo, 0.0)).astype(BF)


def with_edge(inter, mats, edge, cur):
    rows = jnp.concatenate([edge[i * 2 * EDGE : (i + 1) * 2 * EDGE, :] for i in range(RANKS)], axis=1)
    re, im = radiate(rows, cur, EDGE)
    halo = jnp.concatenate([re, im], axis=1).astype(BF)
    return inter[...] + dot(mats[0], halo) + dot(mats[1], halo)


def first_edge_kernel(inter, halo_mat, edge, cur, out):
    out[...] = with_edge(inter, (halo_mat[0, 0], halo_mat[0, 1]), edge, cur)


def multiply(oper, re, im):
    o_re, o_im = oper[:NS, :].astype(F32), oper[NS:, :].astype(F32)
    return (o_re * re - o_im * im).astype(BF), (o_re * im + o_im * re).astype(BF)


def send_kernel(inter, halo_mat, edge, cur, src_pick, oper_slot, slot_ids, out0, out1, out2, out3, rounded):
    whole = with_edge(inter, (halo_mat[1, 0], halo_mat[1, 1]), edge, cur)
    whole = whole.astype(BF)
    rounded[...] = whole
    pick = src_pick[...]
    re, im = dot(whole[:, :BOX], pick), dot(whole[:, BOX:], pick)
    c_re, c_im = multiply(oper_slot[...], re, im)
    for k, out in enumerate((out0, out1, out2, out3)):
        cols = slice(k * CAP, (k + 1) * CAP)
        out[0:NS, :] = c_re[:, cols]
        out[NS : 2 * NS, :] = c_im[:, cols]
        out[2 * NS :, :] = slot_ids[:, cols]


def own_kernel(rounded, own_rows, oper_own, own):
    pick = one_hot(BOX, own_rows[0:1, :])
    re, im = dot(rounded[:, :BOX], pick), dot(rounded[:, BOX:], pick)
    c_re, c_im = multiply(oper_own[...], re, im)
    table = one_hot(BOX, own_rows[1:2, :])
    own[:, :BOX] = dot(c_re, table, NTR)
    own[:, BOX:] = dot(c_im, table, NTR)


def matrix_rows(rad, edge0, edge1, own_mat, edge_mat, steps, out):
    me = lax.axis_index("samp")
    side = 1 - 2 * parity()
    for c in range(2):
        mine, beside = [], []
        for j in steps:
            block = (me + side * j) & (RANKS - 1)
            mine.append(rad[c * NS : (c + 1) * NS, pl.ds(pl.multiple_of(block * CAP, CAP), CAP)])
            rows = pl.ds(pl.multiple_of(block * 2 * EDGE + c * EDGE, 32), EDGE)
            beside.append(jnp.concatenate([edge0[rows, :], edge1[rows, :]], axis=0))
        both = dot(jnp.concatenate(mine, axis=1), own_mat[...], TN)
        both = both + dot(jnp.concatenate(beside, axis=1), edge_mat[...], TN)
        out[:, c * NS : (c + 1) * NS] = (both[:, :NS] + both[:, NS:]).astype(BF)


def matrix_kernel(rad, edge0, edge1, own_mat, edge_mat, out):
    shape = (EDGE, NS)
    t_row, j_row = edge_place(shape, 0)
    t_col, g_col = local_place(shape, 1)
    odd = parity()
    bands = []
    for side, edge in enumerate((edge0, edge1)):
        tail = edge[TAIL:, :].astype(F32)
        cols = (tail[0:8] + tail[8:16]).T[:EDGE]
        base = jnp.where(odd == side, 2 * WIDTH, WIDTH - FD)
        bands.append(band(cols, g_col - j_row + base, t_row == t_col))
    edge_mat[:, :NS], edge_mat[:, NS:] = split(jnp.concatenate(bands, axis=0))
    matrix_rows(rad, edge0, edge1, own_mat, edge_mat, OUTWARD, out)


def far_kernel(own, matrix, got0, got1, got2, got3, out, stack):
    gots = (got0, got1, got2, got3)
    ids = jnp.concatenate([g[2 * NS :, :].astype(F32) for g in gots], axis=1)
    index = (16.0 * ids[0:1] + ids[1:2]).astype(jnp.int32)
    table = one_hot(BOX, index)
    re = own[:, :BOX] + dot(jnp.concatenate([g[0:NS, :] for g in gots], axis=1), table, NTR)
    im = own[:, BOX:] + dot(jnp.concatenate([g[NS : 2 * NS, :] for g in gots], axis=1), table, NTR)
    re, im = re.astype(BF), im.astype(BF)
    stack[0:NS, :BOX] = re
    stack[0:NS, BOX:] = im
    stack[NS:, :BOX] = im
    stack[NS:, BOX:] = -re
    out[...] = dot(matrix[...], stack[...]).astype(BF)


def near_kernel(rad, edge0, edge1, own_mat, edge_mat, stack, inward, keep, matrix):
    matrix_rows(rad, edge0, edge1, own_mat, edge_mat, INWARD + KEPT, matrix)
    cut = len(INWARD) * CAP
    inward[...] = dot(matrix[0:cut, :], stack[...]).astype(BF)
    keep[...] = dot(matrix[cut:, :], stack[...])


def relay_out_kernel(keep, from_inner, out2):
    out2[...] = (keep[CAP : 2 * CAP, :] + from_inner[CAP : 2 * CAP, :].astype(F32)).astype(BF)


def relay_in_kernel(keep, from_inner, from_outer, in3):
    far = from_inner[2 * CAP :, :].astype(F32) + from_outer[CAP:, :].astype(F32)
    in3[...] = (keep[2 * CAP :, :] + far).astype(BF)


def sum_kernel(keep, from_inner, from_outer, out2, in3, out):
    total = keep[0:CAP, :]
    for part in (from_inner[0:CAP, :], from_outer[0:CAP, :], out2[...], in3[...]):
        total = total + part.astype(F32)
    out[0] = total[:, :BOX].astype(BF)
    out[1] = total[:, BOX:].astype(BF)


def call(kernel, outs, *args, scratch=(), flops=10**8, name=None, vmem=24, **kw):
    shapes = [jax.ShapeDtypeStruct(s, d) for s, d in outs]
    moved = sum(a.size * a.dtype.itemsize for a in args) + sum(s.size * s.dtype.itemsize for s in shapes)
    return pl.pallas_call(
        kernel,
        out_shape=shapes,
        scratch_shapes=list(scratch),
        compiler_params=pltpu.CompilerParams(vmem_limit_bytes=vmem * 2**20),
        cost_estimate=pl.CostEstimate(flops=flops, bytes_accessed=moved, transcendentals=0),
        name=name,
        **kw,
    )(*args)


def outward(value, steps):
    groups, count = lax.axis_size("box"), lax.axis_size("samp")
    pairs = []
    for b in range(groups):
        for i in range(count):
            j = (i + (steps if b % 2 == 0 else -steps)) % count
            pairs.append((b * count + i, b * count + j))
    return lax.ppermute(value, ("box", "samp"), pairs)


def across(value):
    groups = lax.axis_size("box")
    return lax.ppermute(value, "box", [(b, b ^ 1) for b in range(groups)])


def sideways(value, steps):
    groups = lax.axis_size("box")
    pairs = [(b, b + steps * (1 if b % 2 else -1)) for b in range(groups)]
    return lax.ppermute(value, "box", [(b, to) for b, to in pairs if 0 <= to < groups])


def on_device(
    currents, radiation, interp, anterp, weights, operators, pair_src, pair_op, pair_target
):
    rad = jnp.transpose(radiation, (0, 2, 3, 1)).reshape(2 * NS, P_SIZE)
    oper = operators.reshape(2 * NS, NOPS)
    weights = weights.reshape(1, NT)
    (edge,) = call(
        edge_kernel,
        [((TAIL + 16, CAP), BF)],
        *(pltpu.with_memory_space_constraint(a, pltpu.HBM) for a in (rad, anterp, weights)),
        scratch=[
            pltpu.VMEM((2 * NS, P_SIZE), BF),
            pltpu.VMEM((2 * WIDTH + 1, FD), F32),
            pltpu.VMEM((1, NT), F32),
            pltpu.SemaphoreType.DMA((EDGE_PARTS + 2,)),
        ],
        name="edge",
        in_specs=[HBM] * 3,
    )
    edge0 = outward(edge, 1)

    (field,) = call(field_kernel, [((NS, 2 * BOX), F32)], rad, currents, flops=10**9, name="field")
    inter, halo_mat, src_pick, oper_slot, slot_ids, oper_own, own_rows, own_mat = call(
        prepare_kernel,
        [
            ((NS, 2 * BOX), F32), ((2, 2, NS, EDGE), BF), ((BOX, SLOTS), BF),
            ((2 * NS, SLOTS), BF), ((16, SLOTS), BF), ((2 * NS, PAIR), BF), ((8, PAIR), jnp.int32),
            ((NS, 2 * NS), BF),
        ],
        field, interp, anterp, weights, pair_src, pair_op, pair_target, oper,
        flops=10**9,
        name="prepare",
    )
    edge0, inter, own_mat = lax.optimization_barrier((edge0, inter, own_mat))
    edge1 = across(edge0)
    (inter,) = call(
        first_edge_kernel, [((NS, 2 * BOX), F32)], inter, halo_mat, edge0, currents,
        flops=4 * 10**8, name="first_edge",
    )
    *buffers, rounded = call(
        send_kernel,
        [((BUF, CAP), BF)] * 4 + [((NS, 2 * BOX), BF)],
        inter, halo_mat, edge1, currents, src_pick, oper_slot, slot_ids,
        flops=4 * 10**8,
        name="send",
    )
    gots = [sideways(b, step) for b, step in zip(buffers, STEPS)]
    (own,) = call(
        own_kernel,
        [((NS, 2 * BOX), F32)],
        rounded, own_rows, oper_own,
        flops=10**9,
        name="own",
    )
    edge_mat, matrix = call(
        matrix_kernel,
        [((2 * EDGE, 2 * NS), BF), ((len(OUTWARD) * CAP, 2 * NS), BF)],
        rad, edge0, edge1, own_mat,
        flops=10**9,
        name="matrix",
    )
    blocks = lambda steps: (steps * CAP, 2 * BOX)
    leaving, stack = call(
        far_kernel,
        [(blocks(len(OUTWARD)), BF), ((2 * NS, 2 * BOX), BF)],
        own, matrix, *gots,
        flops=5 * 10**8,
        name="far",
    )
    from_inner = outward(leaving, 1)
    inward, keep = call(
        near_kernel,
        [(blocks(len(INWARD)), BF), (blocks(len(KEPT)), F32)],
        rad, edge0, edge1, own_mat, edge_mat, stack,
        scratch=[pltpu.VMEM(((len(INWARD) + len(KEPT)) * CAP, 2 * NS), BF)],
        flops=10**9,
        name="near",
    )
    from_outer = outward(inward, -1)
    (out2,) = call(relay_out_kernel, [(blocks(1), BF)], keep, from_inner, name="relay_out")
    from_inner2 = outward(out2, 2)
    (in3,) = call(relay_in_kernel, [(blocks(1), BF)], keep, from_inner, from_outer, name="relay_in")
    from_outer3 = outward(in3, -3)
    (out,) = call(
        sum_kernel,
        [((2, P_SIZE // RANKS, BOX), BF)],
        keep, from_inner, from_outer, from_inner2, from_outer3,
        name="total",
    )
    return out


def solution(mesh):
    return jax.shard_map(
        on_device,
        mesh=mesh,
        in_specs=(
            P(None, None, "box"),
            P(None, None, None, "samp"),
            P(None, "samp"),
            P(None, "samp"),
            P(),
            P(None, None, "samp", None),
            P("box"),
            P("box"),
            P("box"),
        ),
        out_specs=P(None, "samp", "box"),
        check_vma=False,
    )
```

```python
import functools

import jax
import jax.numpy as jnp
from jax import lax
from jax.experimental import pallas as pl
from jax.experimental.pallas import tpu as pltpu
from jax.sharding import PartitionSpec as P

NT = 32
FD = 8
NS = NT * FD
EDGE = 3 * NT
P_SIZE = 1024
NOPS = 316
WIDTH = 3
REACH = 2
BOX = 384
PAIR = 640
CAP = 128
STEPS = (2, -2, 1, -1)
SLOTS = CAP * len(STEPS)
BUF = 2 * NS + 16
RANKS = 8
TAIL = RANKS * 2 * EDGE
OUTWARD = (1, 3, 6)
INWARD = (7, 4)
KEPT = (0, 2, 5)
BF = jnp.bfloat16
HBM = pl.BlockSpec(memory_space=pltpu.HBM)
VMEM = pl.BlockSpec(memory_space=pltpu.VMEM)
EDGE_PARTS = 2
FIELD_PARTS = 4
F32 = jnp.float32

NN = (((1,), (0,)), ((), ()))
NTR = (((1,), (1,)), ((), ()))
TN = (((0,), (0,)), ((), ()))


def dot(a, b, dims=NN):
    return lax.dot_general(a, b, dims, preferred_element_type=F32)


def iota(shape, dim):
    return lax.broadcasted_iota(jnp.int32, shape, dim)


def split(value):
    high = value.astype(BF)
    return high, (value - high.astype(F32)).astype(BF)


def local_place(shape, dim):
    at = iota(shape, dim)
    return at >> 3, at & 7


def edge_place(shape, dim):
    at = iota(shape, dim)
    return at & 31, at >> 5


def band(columns, diff, same):
    total = jnp.zeros(diff.shape, F32)
    for k in range(2 * WIDTH + 1):
        total = jnp.where(diff == k, columns[:, k : k + 1], total)
    return jnp.where(same, total, 0.0)


def exact(a, b, dims=NN):
    return lax.dot_general(a, b, dims, precision=lax.Precision.HIGHEST, preferred_element_type=F32)


def own_columns(coeffs):
    _, f_row = local_place((NS, FD), 0)
    return exact((f_row == iota((NS, FD), 1)).astype(F32), coeffs, NTR)


def sample_weights(weights):
    t_row, _ = local_place((NS, NT), 0)
    same = t_row == iota((NS, NT), 1)
    return jnp.sum(jnp.where(same, weights, 0.0), axis=1, keepdims=True)


def parity():
    return lax.rem(lax.axis_index("box"), 2)


def one_hot(rows, index):
    return (iota((rows, index.shape[1]), 0) == index).astype(BF)


def edge_kernel(rad_all, anterp_all, weights_all, out, rad, anterp, weights, sems):
    parts = EDGE_PARTS
    depth = P_SIZE // parts
    copies = [
        pltpu.make_async_copy(anterp_all, anterp, sems.at[parts]),
        pltpu.make_async_copy(weights_all, weights, sems.at[parts + 1]),
    ]
    for i in range(parts):
        cols = pl.ds(i * depth, depth)
        copies.append(pltpu.make_async_copy(rad_all.at[:, cols], rad.at[:, cols], sems.at[i]))
    for copy in copies:
        copy.start()
    t_row, j_row = edge_place((EDGE, NS), 0)
    t_col, f_col = local_place((EDGE, NS), 1)
    first = jnp.where(parity() == 0, FD - WIDTH, 0)
    pick = jnp.logical_and(t_row == t_col, f_col == j_row + first).astype(BF)
    for i in range(parts):
        copies[2 + i].wait()
        cols = slice(i * depth, (i + 1) * depth)
        for c in range(2):
            picked = dot(pick, rad[c * NS : (c + 1) * NS, cols]).astype(BF)
            for k in range(depth // CAP):
                row = (i * (depth // CAP) + k) * 2 * EDGE + c * EDGE
                out[row : row + EDGE, :] = picked[:, k * CAP : (k + 1) * CAP]
    t_lane, _ = edge_place((NT, CAP), 1)
    _, j_lane = edge_place((FD, CAP), 1)
    copies[0].wait()
    copies[1].wait()
    spread = exact(weights[...], (iota((NT, CAP), 0) == t_lane).astype(F32))
    coeffs = exact(anterp[...], (iota((FD, CAP), 0) == j_lane + first).astype(F32)) * spread
    high, low = split(jnp.concatenate([coeffs, jnp.zeros((1, CAP), F32)], axis=0))
    out[TAIL:, :] = jnp.concatenate([high.astype(F32), low.astype(F32)], axis=0).astype(BF)


def radiate(rad, cur, rows):
    with_re = dot(rad, cur[0])
    with_im = dot(rad, cur[1])
    return with_re[:rows] - with_im[rows:], with_im[:rows] + with_re[rows:]


def field_kernel(rad, cur_all, field, cur, sems):
    depth = P_SIZE // FIELD_PARTS
    copies = []
    for i in range(FIELD_PARTS):
        rows = pl.ds(i * depth, depth)
        copies.append(pltpu.make_async_copy(cur_all.at[:, rows, :], cur.at[:, rows, :], sems.at[i]))
    for copy in copies:
        copy.start()
    with_re, with_im = 0.0, 0.0
    for i in range(FIELD_PARTS):
        copies[i].wait()
        rows = slice(i * depth, (i + 1) * depth)
        with_re = with_re + dot(rad[:, rows], cur[0, rows, :])
        with_im = with_im + dot(rad[:, rows], cur[1, rows, :])
    field[:, :BOX] = with_re[:NS] - with_im[NS:]
    field[:, BOX:] = with_im[:NS] + with_re[NS:]


def prepare_kernel(
    field, interp, anterp, weights, pair_src, pair_op, pair_target, oper,
    inter, halo_mat, src_pick, oper_slot, slot_ids, oper_own, own_rows, own_mat,
):
    columns = own_columns(interp[...])
    shape = (NS, NS)
    t_row, g_row = local_place(shape, 0)
    t_col, f_col = local_place(shape, 1)
    mat_hi, mat_lo = split(band(columns, f_col - g_row + WIDTH, t_row == t_col))
    f_hi, f_lo = split(field[...])
    inter[...] = dot(mat_hi, f_hi) + dot(mat_lo, f_hi) + dot(mat_hi, f_lo)
    shape = (NS, EDGE)
    t_row, g_row = local_place(shape, 0)
    t_col, j_col = edge_place(shape, 1)
    odd = parity()
    for side in range(2):
        base = jnp.where(odd == side, 0, FD + WIDTH)
        mats = split(band(columns, j_col - g_row + base, t_row == t_col))
        for part in range(2):
            halo_mat[side, part] = mats[part]

    shape = (NS, NS)
    t_row, f_row = local_place(shape, 0)
    t_col, g_col = local_place(shape, 1)
    columns = own_columns(anterp[...]) * sample_weights(weights[...])
    own_mat[:, :NS], own_mat[:, NS:] = split(band(columns, g_col - f_row + WIDTH, t_row == t_col))

    src_row, op_row = pair_src[...].reshape(1, PAIR), pair_op[...].reshape(1, PAIR)
    ahead = pair_target[...].reshape(1, PAIR) - lax.axis_index("box") * BOX
    step_of = jnp.full((1, PAIR), -REACH, jnp.int32)
    for k in range(1 - REACH, REACH + 1):
        step_of = step_of + (ahead >= k * BOX).astype(jnp.int32)
    target = ahead - step_of * BOX
    row = iota((8, PAIR), 0)
    own_rows[...] = jnp.where(row == 0, src_row, jnp.where(step_of == 0, target, -1))
    step_of = step_of * (2 * odd - 1)
    digits = jnp.ones((8, PAIR), jnp.int32)
    for k, value in enumerate((src_row, op_row, target)):
        digits = jnp.where(row == 2 * k, value >> 4, digits)
        digits = jnp.where(row == 2 * k + 1, value & 15, digits)
    digits = digits.astype(F32).astype(BF)

    at = iota((8, PAIR), 0)
    cls = jnp.full((1, PAIR), -1, jnp.int32)
    for k, step in enumerate(STEPS):
        cls = jnp.where(step_of == step, k, cls)
    member = (at == cls).astype(BF)
    earlier = (iota((PAIR, PAIR), 0) < iota((PAIR, PAIR), 1)).astype(BF)
    before = dot(member, earlier) * member.astype(F32)
    rank = jnp.sum(before, axis=0, keepdims=True).astype(jnp.int32)
    slot = jnp.where(cls >= 0, cls * CAP + rank, -1)
    chosen = (iota((SLOTS, PAIR), 0) == slot).astype(BF)
    named = dot(digits, chosen, NTR)
    src = (16.0 * named[0:1] + named[1:2]).astype(jnp.int32)
    opn = (16.0 * named[2:3] + named[3:4]).astype(jnp.int32)
    filled = named[6:7] > 0.5
    src_pick[...] = one_hot(BOX, src)
    oper_slot[...] = dot(oper[...], one_hot(NOPS, opn)).astype(BF)
    oper_own[...] = dot(oper[...], one_hot(NOPS, op_row)).astype(BF)
    row = iota((16, SLOTS), 0)
    t_hi = jnp.where(filled, named[4:5], float(BOX // 16))
    t_lo = jnp.where(filled, named[5:6], 0.0)
    slot_ids[...] = jnp.where(row == 0, t_hi, jnp.where(row == 1, t_lo, 0.0)).astype(BF)


def with_edge(inter, mats, edge, cur):
    rows = jnp.concatenate([edge[i * 2 * EDGE : (i + 1) * 2 * EDGE, :] for i in range(RANKS)], axis=1)
    re, im = radiate(rows, cur, EDGE)
    halo = jnp.concatenate([re, im], axis=1).astype(BF)
    return inter[...] + dot(mats[0], halo) + dot(mats[1], halo)


def first_edge_kernel(inter, halo_mat, edge, cur, out):
    out[...] = with_edge(inter, (halo_mat[0, 0], halo_mat[0, 1]), edge, cur)


def multiply(oper, re, im):
    o_re, o_im = oper[:NS, :].astype(F32), oper[NS:, :].astype(F32)
    return (o_re * re - o_im * im).astype(BF), (o_re * im + o_im * re).astype(BF)


def send_kernel(inter, halo_mat, edge, cur, src_pick, oper_slot, slot_ids, out0, out1, out2, out3, rounded):
    whole = with_edge(inter, (halo_mat[1, 0], halo_mat[1, 1]), edge, cur)
    whole = whole.astype(BF)
    rounded[...] = whole
    pick = src_pick[...]
    re, im = dot(whole[:, :BOX], pick), dot(whole[:, BOX:], pick)
    c_re, c_im = multiply(oper_slot[...], re, im)
    for k, out in enumerate((out0, out1, out2, out3)):
        cols = slice(k * CAP, (k + 1) * CAP)
        out[0:NS, :] = c_re[:, cols]
        out[NS : 2 * NS, :] = c_im[:, cols]
        out[2 * NS :, :] = slot_ids[:, cols]


def own_kernel(rounded, own_rows, oper_own, own):
    pick = one_hot(BOX, own_rows[0:1, :])
    re, im = dot(rounded[:, :BOX], pick), dot(rounded[:, BOX:], pick)
    c_re, c_im = multiply(oper_own[...], re, im)
    table = one_hot(BOX, own_rows[1:2, :])
    own[:, :BOX] = dot(c_re, table, NTR)
    own[:, BOX:] = dot(c_im, table, NTR)


def halves(product):
    return product[:, :NS] + product[:, NS:]


def own_terms(rad, own_mat, steps, c):
    me, side = lax.axis_index("samp"), 1 - 2 * parity()
    blocks = []
    for j in steps:
        cols = pl.ds(pl.multiple_of(((me + side * j) & (RANKS - 1)) * CAP, CAP), CAP)
        blocks.append(rad[c * NS : (c + 1) * NS, cols])
    return halves(dot(jnp.concatenate(blocks, axis=1), own_mat[...], TN))


def edge_terms(edge0, edge1, edge_mat, steps, c):
    me, side = lax.axis_index("samp"), 1 - 2 * parity()
    blocks = []
    for j in steps:
        first = ((me + side * j) & (RANKS - 1)) * 2 * EDGE + c * EDGE
        rows = pl.ds(pl.multiple_of(first, 32), EDGE)
        blocks.append(jnp.concatenate([edge0[rows, :], edge1[rows, :]], axis=0))
    return halves(dot(jnp.concatenate(blocks, axis=1), edge_mat[...], TN))


def own_matrix_kernel(rad, own_mat, out):
    for c in range(2):
        out[:, c * NS : (c + 1) * NS] = own_terms(rad, own_mat, OUTWARD, c)


def matrix_kernel(own, edge0, edge1, edge_mat, out):
    shape = (EDGE, NS)
    t_row, j_row = edge_place(shape, 0)
    t_col, g_col = local_place(shape, 1)
    odd = parity()
    bands = []
    for side, edge in enumerate((edge0, edge1)):
        tail = edge[TAIL:, :].astype(F32)
        cols = (tail[0:8] + tail[8:16]).T[:EDGE]
        base = jnp.where(odd == side, 2 * WIDTH, WIDTH - FD)
        bands.append(band(cols, g_col - j_row + base, t_row == t_col))
    edge_mat[:, :NS], edge_mat[:, NS:] = split(jnp.concatenate(bands, axis=0))
    for c in range(2):
        cols = slice(c * NS, (c + 1) * NS)
        out[:, cols] = (own[:, cols] + edge_terms(edge0, edge1, edge_mat, OUTWARD, c)).astype(BF)


def far_kernel(own, matrix, got0, got1, got2, got3, out, stack):
    gots = (got0, got1, got2, got3)
    ids = jnp.concatenate([g[2 * NS :, :].astype(F32) for g in gots], axis=1)
    index = (16.0 * ids[0:1] + ids[1:2]).astype(jnp.int32)
    table = one_hot(BOX, index)
    re = own[:, :BOX] + dot(jnp.concatenate([g[0:NS, :] for g in gots], axis=1), table, NTR)
    im = own[:, BOX:] + dot(jnp.concatenate([g[NS : 2 * NS, :] for g in gots], axis=1), table, NTR)
    re, im = re.astype(BF), im.astype(BF)
    stack[0:NS, :BOX] = re
    stack[0:NS, BOX:] = im
    stack[NS:, :BOX] = im
    stack[NS:, BOX:] = -re
    out[...] = dot(matrix[...], stack[...]).astype(BF)


def near_kernel(rad, edge0, edge1, own_mat, edge_mat, stack, inward, keep, matrix):
    steps = INWARD + KEPT
    for c in range(2):
        terms = own_terms(rad, own_mat, steps, c) + edge_terms(edge0, edge1, edge_mat, steps, c)
        matrix[:, c * NS : (c + 1) * NS] = terms.astype(BF)
    cut = len(INWARD) * CAP
    inward[...] = dot(matrix[0:cut, :], stack[...]).astype(BF)
    keep[...] = dot(matrix[cut:, :], stack[...])


def relay_out_kernel(keep, from_inner, out2):
    out2[...] = (keep[CAP : 2 * CAP, :] + from_inner[CAP : 2 * CAP, :].astype(F32)).astype(BF)


def relay_in_kernel(keep, from_inner, from_outer, in3):
    far = from_inner[2 * CAP :, :].astype(F32) + from_outer[CAP:, :].astype(F32)
    in3[...] = (keep[2 * CAP :, :] + far).astype(BF)


def sum_kernel(keep, from_inner, from_outer, out2, in3, out):
    total = keep[0:CAP, :]
    for part in (from_inner[0:CAP, :], from_outer[0:CAP, :], out2[...], in3[...]):
        total = total + part.astype(F32)
    out[0] = total[:, :BOX].astype(BF)
    out[1] = total[:, BOX:].astype(BF)


def call(kernel, outs, *args, scratch=(), flops=10**8, name=None, vmem=24, **kw):
    shapes = [jax.ShapeDtypeStruct(s, d) for s, d in outs]
    moved = sum(a.size * a.dtype.itemsize for a in args) + sum(s.size * s.dtype.itemsize for s in shapes)
    return pl.pallas_call(
        kernel,
        out_shape=shapes,
        scratch_shapes=list(scratch),
        compiler_params=pltpu.CompilerParams(vmem_limit_bytes=vmem * 2**20),
        cost_estimate=pl.CostEstimate(flops=flops, bytes_accessed=moved, transcendentals=0),
        name=name,
        **kw,
    )(*args)


def outward(value, steps):
    groups, count = lax.axis_size("box"), lax.axis_size("samp")
    pairs = []
    for b in range(groups):
        for i in range(count):
            j = (i + (steps if b % 2 == 0 else -steps)) % count
            pairs.append((b * count + i, b * count + j))
    return lax.ppermute(value, ("box", "samp"), pairs)


def across(value):
    groups = lax.axis_size("box")
    return lax.ppermute(value, "box", [(b, b ^ 1) for b in range(groups)])


def sideways(value, steps):
    groups = lax.axis_size("box")
    pairs = [(b, b + steps * (1 if b % 2 else -1)) for b in range(groups)]
    return lax.ppermute(value, "box", [(b, to) for b, to in pairs if 0 <= to < groups])


def on_device(
    currents, radiation, interp, anterp, weights, operators, pair_src, pair_op, pair_target
):
    rad = jnp.transpose(radiation, (0, 2, 3, 1)).reshape(2 * NS, P_SIZE)
    oper = operators.reshape(2 * NS, NOPS)
    weights = weights.reshape(1, NT)
    edge, rad = call(
        edge_kernel,
        [((TAIL + 16, CAP), BF), (rad.shape, BF)],
        *(pltpu.with_memory_space_constraint(a, pltpu.HBM) for a in (rad, anterp, weights)),
        scratch=[
            pltpu.VMEM((2 * WIDTH + 1, FD), F32),
            pltpu.VMEM((1, NT), F32),
            pltpu.SemaphoreType.DMA((EDGE_PARTS + 2,)),
        ],
        name="edge",
        in_specs=[HBM] * 3,
    )
    edge0 = outward(edge, 1)

    field, currents = call(
        field_kernel,
        [((NS, 2 * BOX), F32), (currents.shape, BF)],
        rad, pltpu.with_memory_space_constraint(currents, pltpu.HBM),
        scratch=[pltpu.SemaphoreType.DMA((FIELD_PARTS,))],
        flops=10**9,
        name="field",
        in_specs=[VMEM, HBM],
    )
    inter, halo_mat, src_pick, oper_slot, slot_ids, oper_own, own_rows, own_mat = call(
        prepare_kernel,
        [
            ((NS, 2 * BOX), F32), ((2, 2, NS, EDGE), BF), ((BOX, SLOTS), BF),
            ((2 * NS, SLOTS), BF), ((16, SLOTS), BF), ((2 * NS, PAIR), BF), ((8, PAIR), jnp.int32),
            ((NS, 2 * NS), BF),
        ],
        field, interp, anterp, weights, pair_src, pair_op, pair_target, oper,
        flops=10**9,
        name="prepare",
    )
    (own_matrix,) = call(
        own_matrix_kernel,
        [((len(OUTWARD) * CAP, 2 * NS), F32)],
        rad, own_mat,
        flops=5 * 10**8,
        name="own_matrix",
    )
    edge0, inter, own_matrix = lax.optimization_barrier((edge0, inter, own_matrix))
    edge1 = across(edge0)
    (inter,) = call(
        first_edge_kernel, [((NS, 2 * BOX), F32)], inter, halo_mat, edge0, currents,
        flops=4 * 10**8, name="first_edge",
    )
    *buffers, rounded = call(
        send_kernel,
        [((BUF, CAP), BF)] * 4 + [((NS, 2 * BOX), BF)],
        inter, halo_mat, edge1, currents, src_pick, oper_slot, slot_ids,
        flops=4 * 10**8,
        name="send",
    )
    gots = [sideways(b, step) for b, step in zip(buffers, STEPS)]
    (own,) = call(
        own_kernel,
        [((NS, 2 * BOX), F32)],
        rounded, own_rows, oper_own,
        flops=10**9,
        name="own",
    )
    edge_mat, matrix = call(
        matrix_kernel,
        [((2 * EDGE, 2 * NS), BF), ((len(OUTWARD) * CAP, 2 * NS), BF)],
        own_matrix, edge0, edge1,
        flops=10**9,
        name="matrix",
    )
    blocks = lambda steps: (steps * CAP, 2 * BOX)
    leaving, stack = call(
        far_kernel,
        [(blocks(len(OUTWARD)), BF), ((2 * NS, 2 * BOX), BF)],
        own, matrix, *gots,
        flops=5 * 10**8,
        name="far",
    )
    from_inner = outward(leaving, 1)
    inward, keep = call(
        near_kernel,
        [(blocks(len(INWARD)), BF), (blocks(len(KEPT)), F32)],
        rad, edge0, edge1, own_mat, edge_mat, stack,
        scratch=[pltpu.VMEM(((len(INWARD) + len(KEPT)) * CAP, 2 * NS), BF)],
        flops=10**9,
        name="near",
    )
    from_outer = outward(inward, -1)
    (out2,) = call(relay_out_kernel, [(blocks(1), BF)], keep, from_inner, name="relay_out")
    from_inner2 = outward(out2, 2)
    (in3,) = call(relay_in_kernel, [(blocks(1), BF)], keep, from_inner, from_outer, name="relay_in")
    from_outer3 = outward(in3, -3)
    (out,) = call(
        sum_kernel,
        [((2, P_SIZE // RANKS, BOX), BF)],
        keep, from_inner, from_outer, from_inner2, from_outer3,
        name="total",
    )
    return out


def solution(mesh):
    return jax.shard_map(
        on_device,
        mesh=mesh,
        in_specs=(
            P(None, None, "box"),
            P(None, None, None, "samp"),
            P(None, "samp"),
            P(None, "samp"),
            P(),
            P(None, None, "samp", None),
            P("box"),
            P("box"),
            P("box"),
        ),
        out_specs=P(None, "samp", "box"),
        check_vma=False,
    )
```

```python
import functools

import jax
import jax.numpy as jnp
from jax import lax
from jax.experimental import pallas as pl
from jax.experimental.pallas import tpu as pltpu
from jax.sharding import PartitionSpec as P

NT = 32
FD = 8
NS = NT * FD
EDGE = 3 * NT
P_SIZE = 1024
NOPS = 316
WIDTH = 3
REACH = 2
BOX = 384
PAIR = 640
CAP = 128
STEPS = (2, -2, 1, -1)
SLOTS = CAP * len(STEPS)
BUF = 2 * NS + 16
RANKS = 8
TAIL = RANKS * 2 * EDGE
OUTWARD = (1, 3, 6)
INWARD = (7, 4)
KEPT = (0, 2, 5)
BF = jnp.bfloat16
HBM = pl.BlockSpec(memory_space=pltpu.HBM)
VMEM = pl.BlockSpec(memory_space=pltpu.VMEM)
EDGE_PARTS = 2
FIELD_PARTS = 4
F32 = jnp.float32

NN = (((1,), (0,)), ((), ()))
NTR = (((1,), (1,)), ((), ()))
TN = (((0,), (0,)), ((), ()))


def dot(a, b, dims=NN):
    return lax.dot_general(a, b, dims, preferred_element_type=F32)


def iota(shape, dim):
    return lax.broadcasted_iota(jnp.int32, shape, dim)


def split(value):
    high = value.astype(BF)
    return high, (value - high.astype(F32)).astype(BF)


def local_place(shape, dim):
    at = iota(shape, dim)
    return at >> 3, at & 7


def edge_place(shape, dim):
    at = iota(shape, dim)
    return at & 31, at >> 5


def band(columns, diff, same):
    total = jnp.zeros(diff.shape, F32)
    for k in range(2 * WIDTH + 1):
        total = jnp.where(diff == k, columns[:, k : k + 1], total)
    return jnp.where(same, total, 0.0)


def exact(a, b, dims=NN):
    return lax.dot_general(a, b, dims, precision=lax.Precision.HIGHEST, preferred_element_type=F32)


def own_columns(coeffs):
    _, f_row = local_place((NS, FD), 0)
    return exact((f_row == iota((NS, FD), 1)).astype(F32), coeffs, NTR)


def sample_weights(weights):
    t_row, _ = local_place((NS, NT), 0)
    same = t_row == iota((NS, NT), 1)
    return jnp.sum(jnp.where(same, weights, 0.0), axis=1, keepdims=True)


def parity():
    return lax.rem(lax.axis_index("box"), 2)


def one_hot(rows, index):
    return (iota((rows, index.shape[1]), 0) == index).astype(BF)


def edge_kernel(rad_all, anterp_all, weights_all, out, rad, anterp, weights, sems):
    parts = EDGE_PARTS
    depth = P_SIZE // parts
    copies = [
        pltpu.make_async_copy(anterp_all, anterp, sems.at[parts]),
        pltpu.make_async_copy(weights_all, weights, sems.at[parts + 1]),
    ]
    for i in range(parts):
        cols = pl.ds(i * depth, depth)
        copies.append(pltpu.make_async_copy(rad_all.at[:, cols], rad.at[:, cols], sems.at[i]))
    for copy in copies:
        copy.start()
    t_row, j_row = edge_place((EDGE, NS), 0)
    t_col, f_col = local_place((EDGE, NS), 1)
    first = jnp.where(parity() == 0, FD - WIDTH, 0)
    pick = jnp.logical_and(t_row == t_col, f_col == j_row + first).astype(BF)
    for i in range(parts):
        copies[2 + i].wait()
        cols = slice(i * depth, (i + 1) * depth)
        for c in range(2):
            picked = dot(pick, rad[c * NS : (c + 1) * NS, cols]).astype(BF)
            for k in range(depth // CAP):
                row = (i * (depth // CAP) + k) * 2 * EDGE + c * EDGE
                out[row : row + EDGE, :] = picked[:, k * CAP : (k + 1) * CAP]
    t_lane, _ = edge_place((NT, CAP), 1)
    _, j_lane = edge_place((FD, CAP), 1)
    copies[0].wait()
    copies[1].wait()
    spread = exact(weights[...], (iota((NT, CAP), 0) == t_lane).astype(F32))
    coeffs = exact(anterp[...], (iota((FD, CAP), 0) == j_lane + first).astype(F32)) * spread
    high, low = split(jnp.concatenate([coeffs, jnp.zeros((1, CAP), F32)], axis=0))
    out[TAIL:, :] = jnp.concatenate([high.astype(F32), low.astype(F32)], axis=0).astype(BF)


def radiate(rad, cur, rows):
    with_re = dot(rad, cur[0])
    with_im = dot(rad, cur[1])
    return with_re[:rows] - with_im[rows:], with_im[:rows] + with_re[rows:]


def field_kernel(rad, cur_all, field, cur, sems):
    depth = P_SIZE // FIELD_PARTS
    copies = []
    for i in range(FIELD_PARTS):
        rows = pl.ds(i * depth, depth)
        copies.append(pltpu.make_async_copy(cur_all.at[:, rows, :], cur.at[:, rows, :], sems.at[i]))
    for copy in copies:
        copy.start()
    with_re, with_im = 0.0, 0.0
    for i in range(FIELD_PARTS):
        copies[i].wait()
        rows = slice(i * depth, (i + 1) * depth)
        with_re = with_re + dot(rad[:, rows], cur[0, rows, :])
        with_im = with_im + dot(rad[:, rows], cur[1, rows, :])
    field[:, :BOX] = with_re[:NS] - with_im[NS:]
    field[:, BOX:] = with_im[:NS] + with_re[NS:]


def prepare_kernel(
    field, interp, anterp, weights, pair_src, pair_op, pair_target, oper,
    inter, halo_mat, src_pick, oper_slot, slot_ids, oper_own, own_pick, own_table, own_mat,
):
    columns = own_columns(interp[...])
    shape = (NS, NS)
    t_row, g_row = local_place(shape, 0)
    t_col, f_col = local_place(shape, 1)
    mat_hi, mat_lo = split(band(columns, f_col - g_row + WIDTH, t_row == t_col))
    f_hi, f_lo = split(field[...])
    inter[...] = dot(mat_hi, f_hi) + dot(mat_lo, f_hi) + dot(mat_hi, f_lo)
    shape = (NS, EDGE)
    t_row, g_row = local_place(shape, 0)
    t_col, j_col = edge_place(shape, 1)
    odd = parity()
    for side in range(2):
        base = jnp.where(odd == side, 0, FD + WIDTH)
        mats = split(band(columns, j_col - g_row + base, t_row == t_col))
        for part in range(2):
            halo_mat[side, part] = mats[part]

    shape = (NS, NS)
    t_row, f_row = local_place(shape, 0)
    t_col, g_col = local_place(shape, 1)
    columns = own_columns(anterp[...]) * sample_weights(weights[...])
    own_mat[:, :NS], own_mat[:, NS:] = split(band(columns, g_col - f_row + WIDTH, t_row == t_col))

    src_row, op_row = pair_src[...].reshape(1, PAIR), pair_op[...].reshape(1, PAIR)
    ahead = pair_target[...].reshape(1, PAIR) - lax.axis_index("box") * BOX
    step_of = jnp.full((1, PAIR), -REACH, jnp.int32)
    for k in range(1 - REACH, REACH + 1):
        step_of = step_of + (ahead >= k * BOX).astype(jnp.int32)
    target = ahead - step_of * BOX
    row = iota((8, PAIR), 0)
    own_pick[...] = one_hot(BOX, src_row)
    own_table[...] = one_hot(BOX, jnp.where(step_of == 0, target, -1))
    step_of = step_of * (2 * odd - 1)
    digits = jnp.ones((8, PAIR), jnp.int32)
    for k, value in enumerate((src_row, op_row, target)):
        digits = jnp.where(row == 2 * k, value >> 4, digits)
        digits = jnp.where(row == 2 * k + 1, value & 15, digits)
    digits = digits.astype(F32).astype(BF)

    at = iota((8, PAIR), 0)
    cls = jnp.full((1, PAIR), -1, jnp.int32)
    for k, step in enumerate(STEPS):
        cls = jnp.where(step_of == step, k, cls)
    member = (at == cls).astype(BF)
    earlier = (iota((PAIR, PAIR), 0) < iota((PAIR, PAIR), 1)).astype(BF)
    before = dot(member, earlier) * member.astype(F32)
    rank = jnp.sum(before, axis=0, keepdims=True).astype(jnp.int32)
    slot = jnp.where(cls >= 0, cls * CAP + rank, -1)
    chosen = (iota((SLOTS, PAIR), 0) == slot).astype(BF)
    named = dot(digits, chosen, NTR)
    src = (16.0 * named[0:1] + named[1:2]).astype(jnp.int32)
    opn = (16.0 * named[2:3] + named[3:4]).astype(jnp.int32)
    filled = named[6:7] > 0.5
    src_pick[...] = one_hot(BOX, src)
    oper_slot[...] = dot(oper[...], one_hot(NOPS, opn)).astype(BF)
    oper_own[...] = dot(oper[...], one_hot(NOPS, op_row)).astype(BF)
    row = iota((16, SLOTS), 0)
    t_hi = jnp.where(filled, named[4:5], float(BOX // 16))
    t_lo = jnp.where(filled, named[5:6], 0.0)
    slot_ids[...] = jnp.where(row == 0, t_hi, jnp.where(row == 1, t_lo, 0.0)).astype(BF)


def with_edge(inter, mats, edge, cur):
    rows = jnp.concatenate([edge[i * 2 * EDGE : (i + 1) * 2 * EDGE, :] for i in range(RANKS)], axis=1)
    re, im = radiate(rows, cur, EDGE)
    halo = jnp.concatenate([re, im], axis=1).astype(BF)
    return inter[...] + dot(mats[0], halo) + dot(mats[1], halo)


def first_edge_kernel(inter, halo_mat, edge, cur, out):
    out[...] = with_edge(inter, (halo_mat[0, 0], halo_mat[0, 1]), edge, cur)


def multiply(oper, re, im):
    o_re, o_im = oper[:NS, :].astype(F32), oper[NS:, :].astype(F32)
    return (o_re * re - o_im * im).astype(BF), (o_re * im + o_im * re).astype(BF)


def send_kernel(inter, halo_mat, edge, cur, src_pick, oper_slot, slot_ids, out0, out1, out2, out3, rounded):
    whole = with_edge(inter, (halo_mat[1, 0], halo_mat[1, 1]), edge, cur)
    whole = whole.astype(BF)
    rounded[...] = whole
    pick = src_pick[...]
    re, im = dot(whole[:, :BOX], pick), dot(whole[:, BOX:], pick)
    c_re, c_im = multiply(oper_slot[...], re, im)
    for k, out in enumerate((out0, out1, out2, out3)):
        cols = slice(k * CAP, (k + 1) * CAP)
        out[0:NS, :] = c_re[:, cols]
        out[NS : 2 * NS, :] = c_im[:, cols]
        out[2 * NS :, :] = slot_ids[:, cols]


def own_kernel(rounded, own_pick, own_table, oper_own, own):
    pick = own_pick[...]
    re, im = dot(rounded[:, :BOX], pick), dot(rounded[:, BOX:], pick)
    c_re, c_im = multiply(oper_own[...], re, im)
    table = own_table[...]
    own[:, :BOX] = dot(c_re, table, NTR)
    own[:, BOX:] = dot(c_im, table, NTR)


def halves(product):
    return product[:, :NS] + product[:, NS:]


def own_terms(rad, own_mat, steps, c):
    me, side = lax.axis_index("samp"), 1 - 2 * parity()
    blocks = []
    for j in steps:
        cols = pl.ds(pl.multiple_of(((me + side * j) & (RANKS - 1)) * CAP, CAP), CAP)
        blocks.append(rad[c * NS : (c + 1) * NS, cols])
    return halves(dot(jnp.concatenate(blocks, axis=1), own_mat[...], TN))


def edge_terms(edge0, edge1, edge_mat, steps, c):
    me, side = lax.axis_index("samp"), 1 - 2 * parity()
    blocks = []
    for j in steps:
        first = ((me + side * j) & (RANKS - 1)) * 2 * EDGE + c * EDGE
        rows = pl.ds(pl.multiple_of(first, 32), EDGE)
        blocks.append(jnp.concatenate([edge0[rows, :], edge1[rows, :]], axis=0))
    return halves(dot(jnp.concatenate(blocks, axis=1), edge_mat[...], TN))


def own_matrix_kernel(rad, own_mat, out):
    for c in range(2):
        out[:, c * NS : (c + 1) * NS] = own_terms(rad, own_mat, OUTWARD, c)


def matrix_kernel(own, edge0, edge1, edge_mat, out):
    shape = (EDGE, NS)
    t_row, j_row = edge_place(shape, 0)
    t_col, g_col = local_place(shape, 1)
    odd = parity()
    bands = []
    for side, edge in enumerate((edge0, edge1)):
        tail = edge[TAIL:, :].astype(F32)
        cols = (tail[0:8] + tail[8:16]).T[:EDGE]
        base = jnp.where(odd == side, 2 * WIDTH, WIDTH - FD)
        bands.append(band(cols, g_col - j_row + base, t_row == t_col))
    edge_mat[:, :NS], edge_mat[:, NS:] = split(jnp.concatenate(bands, axis=0))
    for c in range(2):
        cols = slice(c * NS, (c + 1) * NS)
        out[:, cols] = (own[:, cols] + edge_terms(edge0, edge1, edge_mat, OUTWARD, c)).astype(BF)


def far_kernel(own, matrix, got0, got1, got2, got3, out, stack):
    gots = (got0, got1, got2, got3)
    ids = jnp.concatenate([g[2 * NS :, :].astype(F32) for g in gots], axis=1)
    index = (16.0 * ids[0:1] + ids[1:2]).astype(jnp.int32)
    table = one_hot(BOX, index)
    re = own[:, :BOX] + dot(jnp.concatenate([g[0:NS, :] for g in gots], axis=1), table, NTR)
    im = own[:, BOX:] + dot(jnp.concatenate([g[NS : 2 * NS, :] for g in gots], axis=1), table, NTR)
    re, im = re.astype(BF), im.astype(BF)
    stack[0:NS, :BOX] = re
    stack[0:NS, BOX:] = im
    stack[NS:, :BOX] = im
    stack[NS:, BOX:] = -re
    out[...] = dot(matrix[...], stack[...]).astype(BF)


def near_kernel(rad, edge0, edge1, own_mat, edge_mat, stack, inward, keep, matrix):
    steps = INWARD + KEPT
    for c in range(2):
        terms = own_terms(rad, own_mat, steps, c) + edge_terms(edge0, edge1, edge_mat, steps, c)
        matrix[:, c * NS : (c + 1) * NS] = terms.astype(BF)
    cut = len(INWARD) * CAP
    inward[...] = dot(matrix[0:cut, :], stack[...]).astype(BF)
    keep[...] = dot(matrix[cut:, :], stack[...])


def relay_out_kernel(keep, from_inner, out2):
    out2[...] = (keep[CAP : 2 * CAP, :] + from_inner[CAP : 2 * CAP, :].astype(F32)).astype(BF)


def relay_in_kernel(keep, from_inner, from_outer, in3):
    far = from_inner[2 * CAP :, :].astype(F32) + from_outer[CAP:, :].astype(F32)
    in3[...] = (keep[2 * CAP :, :] + far).astype(BF)


def sum_kernel(keep, from_inner, from_outer, out2, in3, out):
    total = keep[0:CAP, :]
    for part in (from_inner[0:CAP, :], from_outer[0:CAP, :], out2[...], in3[...]):
        total = total + part.astype(F32)
    out[0] = total[:, :BOX].astype(BF)
    out[1] = total[:, BOX:].astype(BF)


def call(kernel, outs, *args, scratch=(), flops=10**8, name=None, vmem=24, **kw):
    shapes = [jax.ShapeDtypeStruct(s, d) for s, d in outs]
    moved = sum(a.size * a.dtype.itemsize for a in args) + sum(s.size * s.dtype.itemsize for s in shapes)
    return pl.pallas_call(
        kernel,
        out_shape=shapes,
        scratch_shapes=list(scratch),
        compiler_params=pltpu.CompilerParams(vmem_limit_bytes=vmem * 2**20),
        cost_estimate=pl.CostEstimate(flops=flops, bytes_accessed=moved, transcendentals=0),
        name=name,
        **kw,
    )(*args)


def outward(value, steps):
    groups, count = lax.axis_size("box"), lax.axis_size("samp")
    pairs = []
    for b in range(groups):
        for i in range(count):
            j = (i + (steps if b % 2 == 0 else -steps)) % count
            pairs.append((b * count + i, b * count + j))
    return lax.ppermute(value, ("box", "samp"), pairs)


def across(value):
    groups = lax.axis_size("box")
    return lax.ppermute(value, "box", [(b, b ^ 1) for b in range(groups)])


def sideways(value, steps):
    groups = lax.axis_size("box")
    pairs = [(b, b + steps * (1 if b % 2 else -1)) for b in range(groups)]
    return lax.ppermute(value, "box", [(b, to) for b, to in pairs if 0 <= to < groups])


def on_device(
    currents, radiation, interp, anterp, weights, operators, pair_src, pair_op, pair_target
):
    rad = jnp.transpose(radiation, (0, 2, 3, 1)).reshape(2 * NS, P_SIZE)
    oper = operators.reshape(2 * NS, NOPS)
    weights = weights.reshape(1, NT)
    edge, rad = call(
        edge_kernel,
        [((TAIL + 16, CAP), BF), (rad.shape, BF)],
        *(pltpu.with_memory_space_constraint(a, pltpu.HBM) for a in (rad, anterp, weights)),
        scratch=[
            pltpu.VMEM((2 * WIDTH + 1, FD), F32),
            pltpu.VMEM((1, NT), F32),
            pltpu.SemaphoreType.DMA((EDGE_PARTS + 2,)),
        ],
        name="edge",
        in_specs=[HBM] * 3,
    )
    edge0 = outward(edge, 1)

    field, currents = call(
        field_kernel,
        [((NS, 2 * BOX), F32), (currents.shape, BF)],
        rad, pltpu.with_memory_space_constraint(currents, pltpu.HBM),
        scratch=[pltpu.SemaphoreType.DMA((FIELD_PARTS,))],
        flops=10**9,
        name="field",
        in_specs=[VMEM, HBM],
    )
    inter, halo_mat, src_pick, oper_slot, slot_ids, oper_own, own_pick, own_table, own_mat = call(
        prepare_kernel,
        [
            ((NS, 2 * BOX), F32), ((2, 2, NS, EDGE), BF), ((BOX, SLOTS), BF),
            ((2 * NS, SLOTS), BF), ((16, SLOTS), BF), ((2 * NS, PAIR), BF), ((BOX, PAIR), BF), ((BOX, PAIR), BF),
            ((NS, 2 * NS), BF),
        ],
        field, interp, anterp, weights, pair_src, pair_op, pair_target, oper,
        flops=10**9,
        name="prepare",
    )
    (own_matrix,) = call(
        own_matrix_kernel,
        [((len(OUTWARD) * CAP, 2 * NS), F32)],
        rad, own_mat,
        flops=5 * 10**8,
        name="own_matrix",
    )
    edge0, inter, own_matrix = lax.optimization_barrier((edge0, inter, own_matrix))
    edge1 = across(edge0)
    (inter,) = call(
        first_edge_kernel, [((NS, 2 * BOX), F32)], inter, halo_mat, edge0, currents,
        flops=4 * 10**8, name="first_edge",
    )
    *buffers, rounded = call(
        send_kernel,
        [((BUF, CAP), BF)] * 4 + [((NS, 2 * BOX), BF)],
        inter, halo_mat, edge1, currents, src_pick, oper_slot, slot_ids,
        flops=4 * 10**8,
        name="send",
    )
    gots = [sideways(b, step) for b, step in zip(buffers, STEPS)]
    (own,) = call(
        own_kernel,
        [((NS, 2 * BOX), F32)],
        rounded, own_pick, own_table, oper_own,
        flops=10**9,
        name="own",
    )
    edge_mat, matrix = call(
        matrix_kernel,
        [((2 * EDGE, 2 * NS), BF), ((len(OUTWARD) * CAP, 2 * NS), BF)],
        own_matrix, edge0, edge1,
        flops=10**9,
        name="matrix",
    )
    blocks = lambda steps: (steps * CAP, 2 * BOX)
    leaving, stack = call(
        far_kernel,
        [(blocks(len(OUTWARD)), BF), ((2 * NS, 2 * BOX), BF)],
        own, matrix, *gots,
        flops=5 * 10**8,
        name="far",
    )
    from_inner = outward(leaving, 1)
    inward, keep = call(
        near_kernel,
        [(blocks(len(INWARD)), BF), (blocks(len(KEPT)), F32)],
        rad, edge0, edge1, own_mat, edge_mat, stack,
        scratch=[pltpu.VMEM(((len(INWARD) + len(KEPT)) * CAP, 2 * NS), BF)],
        flops=10**9,
        name="near",
    )
    from_outer = outward(inward, -1)
    (out2,) = call(relay_out_kernel, [(blocks(1), BF)], keep, from_inner, name="relay_out")
    from_inner2 = outward(out2, 2)
    (in3,) = call(relay_in_kernel, [(blocks(1), BF)], keep, from_inner, from_outer, name="relay_in")
    from_outer3 = outward(in3, -3)
    (out,) = call(
        sum_kernel,
        [((2, P_SIZE // RANKS, BOX), BF)],
        keep, from_inner, from_outer, from_inner2, from_outer3,
        name="total",
    )
    return out


def solution(mesh):
    return jax.shard_map(
        on_device,
        mesh=mesh,
        in_specs=(
            P(None, None, "box"),
            P(None, None, None, "samp"),
            P(None, "samp"),
            P(None, "samp"),
            P(),
            P(None, None, "samp", None),
            P("box"),
            P("box"),
            P("box"),
        ),
        out_specs=P(None, "samp", "box"),
        check_vma=False,
    )
```

```python
import functools

import jax
import jax.numpy as jnp
from jax import lax
from jax.experimental import pallas as pl
from jax.experimental.pallas import tpu as pltpu
from jax.sharding import PartitionSpec as P

NT = 32
FD = 8
NS = NT * FD
EDGE = 3 * NT
P_SIZE = 1024
NOPS = 316
WIDTH = 3
REACH = 2
BOX = 384
PAIR = 640
CAP = 128
STEPS = (2, -2, 1, -1)
SLOTS = CAP * len(STEPS)
BUF = 2 * NS + 16
RANKS = 8
TAIL = RANKS * 2 * EDGE
OUTWARD = (1, 3, 6)
INWARD = (7, 4)
KEPT = (0, 2, 5)
BF = jnp.bfloat16
HBM = pl.BlockSpec(memory_space=pltpu.HBM)
EDGE_PARTS = 2
F32 = jnp.float32

NN = (((1,), (0,)), ((), ()))
NTR = (((1,), (1,)), ((), ()))
TN = (((0,), (0,)), ((), ()))


def dot(a, b, dims=NN):
    return lax.dot_general(a, b, dims, preferred_element_type=F32)


def iota(shape, dim):
    return lax.broadcasted_iota(jnp.int32, shape, dim)


def split(value):
    high = value.astype(BF)
    return high, (value - high.astype(F32)).astype(BF)


def local_place(shape, dim):
    at = iota(shape, dim)
    return at >> 3, at & 7


def edge_place(shape, dim):
    at = iota(shape, dim)
    return at & 31, at >> 5


def band(columns, diff, same):
    total = jnp.zeros(diff.shape, F32)
    for k in range(2 * WIDTH + 1):
        total = jnp.where(diff == k, columns[:, k : k + 1], total)
    return jnp.where(same, total, 0.0)


def exact(a, b, dims=NN):
    return lax.dot_general(a, b, dims, precision=lax.Precision.HIGHEST, preferred_element_type=F32)


def own_columns(coeffs):
    _, f_row = local_place((NS, FD), 0)
    return exact((f_row == iota((NS, FD), 1)).astype(F32), coeffs, NTR)


def sample_weights(weights):
    t_row, _ = local_place((NS, NT), 0)
    same = t_row == iota((NS, NT), 1)
    return jnp.sum(jnp.where(same, weights, 0.0), axis=1, keepdims=True)


def parity():
    return lax.rem(lax.axis_index("box"), 2)


def one_hot(rows, index):
    return (iota((rows, index.shape[1]), 0) == index).astype(BF)


def edge_kernel(rad_all, anterp_all, weights_all, out, rad, anterp, weights, sems):
    parts = EDGE_PARTS
    depth = P_SIZE // parts
    copies = [
        pltpu.make_async_copy(anterp_all, anterp, sems.at[parts]),
        pltpu.make_async_copy(weights_all, weights, sems.at[parts + 1]),
    ]
    for i in range(parts):
        cols = pl.ds(i * depth, depth)
        copies.append(pltpu.make_async_copy(rad_all.at[:, cols], rad.at[:, cols], sems.at[i]))
    for copy in copies:
        copy.start()
    t_row, j_row = edge_place((EDGE, NS), 0)
    t_col, f_col = local_place((EDGE, NS), 1)
    first = jnp.where(parity() == 0, FD - WIDTH, 0)
    pick = jnp.logical_and(t_row == t_col, f_col == j_row + first).astype(BF)
    for i in range(parts):
        copies[2 + i].wait()
        cols = slice(i * depth, (i + 1) * depth)
        for c in range(2):
            picked = dot(pick, rad[c * NS : (c + 1) * NS, cols]).astype(BF)
            for k in range(depth // CAP):
                row = (i * (depth // CAP) + k) * 2 * EDGE + c * EDGE
                out[row : row + EDGE, :] = picked[:, k * CAP : (k + 1) * CAP]
    t_lane, _ = edge_place((NT, CAP), 1)
    _, j_lane = edge_place((FD, CAP), 1)
    copies[0].wait()
    copies[1].wait()
    spread = exact(weights[...], (iota((NT, CAP), 0) == t_lane).astype(F32))
    coeffs = exact(anterp[...], (iota((FD, CAP), 0) == j_lane + first).astype(F32)) * spread
    high, low = split(jnp.concatenate([coeffs, jnp.zeros((1, CAP), F32)], axis=0))
    out[TAIL:, :] = jnp.concatenate([high.astype(F32), low.astype(F32)], axis=0).astype(BF)


def radiate(rad, cur, rows):
    with_re = dot(rad, cur[0])
    with_im = dot(rad, cur[1])
    return with_re[:rows] - with_im[rows:], with_im[:rows] + with_re[rows:]


def field_kernel(rad, cur, field):
    re, im = radiate(rad[...], cur, NS)
    field[:, :BOX] = re
    field[:, BOX:] = im


def prepare_kernel(
    field, interp, anterp, weights, pair_src, pair_op, pair_target, oper,
    inter, halo_mat, src_pick, oper_slot, slot_ids, oper_own, own_rows, own_mat,
):
    columns = own_columns(interp[...])
    shape = (NS, NS)
    t_row, g_row = local_place(shape, 0)
    t_col, f_col = local_place(shape, 1)
    mat_hi, mat_lo = split(band(columns, f_col - g_row + WIDTH, t_row == t_col))
    f_hi, f_lo = split(field[...])
    inter[...] = dot(mat_hi, f_hi) + dot(mat_lo, f_hi) + dot(mat_hi, f_lo)
    shape = (NS, EDGE)
    t_row, g_row = local_place(shape, 0)
    t_col, j_col = edge_place(shape, 1)
    odd = parity()
    for side in range(2):
        base = jnp.where(odd == side, 0, FD + WIDTH)
        mats = split(band(columns, j_col - g_row + base, t_row == t_col))
        for part in range(2):
            halo_mat[side, part] = mats[part]

    shape = (NS, NS)
    t_row, f_row = local_place(shape, 0)
    t_col, g_col = local_place(shape, 1)
    columns = own_columns(anterp[...]) * sample_weights(weights[...])
    own_mat[:, :NS], own_mat[:, NS:] = split(band(columns, g_col - f_row + WIDTH, t_row == t_col))

    src_row, op_row = pair_src[...].reshape(1, PAIR), pair_op[...].reshape(1, PAIR)
    ahead = pair_target[...].reshape(1, PAIR) - lax.axis_index("box") * BOX
    step_of = jnp.full((1, PAIR), -REACH, jnp.int32)
    for k in range(1 - REACH, REACH + 1):
        step_of = step_of + (ahead >= k * BOX).astype(jnp.int32)
    target = ahead - step_of * BOX
    row = iota((8, PAIR), 0)
    own_rows[...] = jnp.where(row == 0, src_row, jnp.where(step_of == 0, target, -1))
    step_of = step_of * (2 * odd - 1)
    digits = jnp.ones((8, PAIR), jnp.int32)
    for k, value in enumerate((src_row, op_row, target)):
        digits = jnp.where(row == 2 * k, value >> 4, digits)
        digits = jnp.where(row == 2 * k + 1, value & 15, digits)
    digits = digits.astype(F32).astype(BF)

    at = iota((8, PAIR), 0)
    cls = jnp.full((1, PAIR), -1, jnp.int32)
    for k, step in enumerate(STEPS):
        cls = jnp.where(step_of == step, k, cls)
    member = (at == cls).astype(BF)
    earlier = (iota((PAIR, PAIR), 0) < iota((PAIR, PAIR), 1)).astype(BF)
    before = dot(member, earlier) * member.astype(F32)
    rank = jnp.sum(before, axis=0, keepdims=True).astype(jnp.int32)
    slot = jnp.where(cls >= 0, cls * CAP + rank, -1)
    chosen = (iota((SLOTS, PAIR), 0) == slot).astype(BF)
    named = dot(digits, chosen, NTR)
    src = (16.0 * named[0:1] + named[1:2]).astype(jnp.int32)
    opn = (16.0 * named[2:3] + named[3:4]).astype(jnp.int32)
    filled = named[6:7] > 0.5
    src_pick[...] = one_hot(BOX, src)
    oper_slot[...] = dot(oper[...], one_hot(NOPS, opn)).astype(BF)
    oper_own[...] = dot(oper[...], one_hot(NOPS, op_row)).astype(BF)
    row = iota((16, SLOTS), 0)
    t_hi = jnp.where(filled, named[4:5], float(BOX // 16))
    t_lo = jnp.where(filled, named[5:6], 0.0)
    slot_ids[...] = jnp.where(row == 0, t_hi, jnp.where(row == 1, t_lo, 0.0)).astype(BF)


def with_edge(inter, mats, edge, cur):
    rows = jnp.concatenate([edge[i * 2 * EDGE : (i + 1) * 2 * EDGE, :] for i in range(RANKS)], axis=1)
    re, im = radiate(rows, cur, EDGE)
    halo = jnp.concatenate([re, im], axis=1).astype(BF)
    return inter[...] + dot(mats[0], halo) + dot(mats[1], halo)


def first_edge_kernel(inter, halo_mat, edge, cur, out):
    out[...] = with_edge(inter, (halo_mat[0, 0], halo_mat[0, 1]), edge, cur)


def multiply(oper, re, im):
    o_re, o_im = oper[:NS, :].astype(F32), oper[NS:, :].astype(F32)
    return (o_re * re - o_im * im).astype(BF), (o_re * im + o_im * re).astype(BF)


def send_kernel(inter, halo_mat, edge, cur, src_pick, oper_slot, slot_ids, out0, out1, out2, out3, rounded):
    whole = with_edge(inter, (halo_mat[1, 0], halo_mat[1, 1]), edge, cur)
    whole = whole.astype(BF)
    rounded[...] = whole
    pick = src_pick[...]
    re, im = dot(whole[:, :BOX], pick), dot(whole[:, BOX:], pick)
    c_re, c_im = multiply(oper_slot[...], re, im)
    for k, out in enumerate((out0, out1, out2, out3)):
        cols = slice(k * CAP, (k + 1) * CAP)
        out[0:NS, :] = c_re[:, cols]
        out[NS : 2 * NS, :] = c_im[:, cols]
        out[2 * NS :, :] = slot_ids[:, cols]


def own_kernel(rounded, own_rows, oper_own, own):
    pick = one_hot(BOX, own_rows[0:1, :])
    re, im = dot(rounded[:, :BOX], pick), dot(rounded[:, BOX:], pick)
    c_re, c_im = multiply(oper_own[...], re, im)
    table = one_hot(BOX, own_rows[1:2, :])
    own[:, :BOX] = dot(c_re, table, NTR)
    own[:, BOX:] = dot(c_im, table, NTR)


def matrix_rows(rad, edge0, edge1, own_mat, edge_mat, steps, out):
    me = lax.axis_index("samp")
    side = 1 - 2 * parity()
    for c in range(2):
        mine, beside = [], []
        for j in steps:
            block = (me + side * j) & (RANKS - 1)
            mine.append(rad[c * NS : (c + 1) * NS, pl.ds(pl.multiple_of(block * CAP, CAP), CAP)])
            rows = pl.ds(pl.multiple_of(block * 2 * EDGE + c * EDGE, 32), EDGE)
            beside.append(jnp.concatenate([edge0[rows, :], edge1[rows, :]], axis=0))
        both = dot(jnp.concatenate(mine, axis=1), own_mat[...], TN)
        both = both + dot(jnp.concatenate(beside, axis=1), edge_mat[...], TN)
        out[:, c * NS : (c + 1) * NS] = (both[:, :NS] + both[:, NS:]).astype(BF)


def matrix_kernel(rad, edge0, edge1, own_mat, edge_mat, out):
    shape = (EDGE, NS)
    t_row, j_row = edge_place(shape, 0)
    t_col, g_col = local_place(shape, 1)
    odd = parity()
    bands = []
    for side, edge in enumerate((edge0, edge1)):
        tail = edge[TAIL:, :].astype(F32)
        cols = (tail[0:8] + tail[8:16]).T[:EDGE]
        base = jnp.where(odd == side, 2 * WIDTH, WIDTH - FD)
        bands.append(band(cols, g_col - j_row + base, t_row == t_col))
    edge_mat[:, :NS], edge_mat[:, NS:] = split(jnp.concatenate(bands, axis=0))
    matrix_rows(rad, edge0, edge1, own_mat, edge_mat, OUTWARD, out)


def far_kernel(own, matrix, got0, got1, got2, got3, out, stack):
    gots = (got0, got1, got2, got3)
    ids = jnp.concatenate([g[2 * NS :, :].astype(F32) for g in gots], axis=1)
    index = (16.0 * ids[0:1] + ids[1:2]).astype(jnp.int32)
    table = one_hot(BOX, index)
    re = own[:, :BOX] + dot(jnp.concatenate([g[0:NS, :] for g in gots], axis=1), table, NTR)
    im = own[:, BOX:] + dot(jnp.concatenate([g[NS : 2 * NS, :] for g in gots], axis=1), table, NTR)
    re, im = re.astype(BF), im.astype(BF)
    stack[0:NS, :BOX] = re
    stack[0:NS, BOX:] = im
    stack[NS:, :BOX] = im
    stack[NS:, BOX:] = -re
    out[...] = dot(matrix[...], stack[...]).astype(BF)


def near_kernel(rad, edge0, edge1, own_mat, edge_mat, stack, inward, keep, matrix):
    matrix_rows(rad, edge0, edge1, own_mat, edge_mat, INWARD + KEPT, matrix)
    cut = len(INWARD) * CAP
    inward[...] = dot(matrix[0:cut, :], stack[...]).astype(BF)
    keep[...] = dot(matrix[cut:, :], stack[...])


def relay_out_kernel(keep, from_inner, out2):
    out2[...] = (keep[CAP : 2 * CAP, :] + from_inner[CAP : 2 * CAP, :].astype(F32)).astype(BF)


def relay_in_kernel(keep, from_inner, from_outer, in3):
    far = from_inner[2 * CAP :, :].astype(F32) + from_outer[CAP:, :].astype(F32)
    in3[...] = (keep[2 * CAP :, :] + far).astype(BF)


def sum_kernel(keep, from_inner, from_outer, out2, in3, out):
    total = keep[0:CAP, :]
    for part in (from_inner[0:CAP, :], from_outer[0:CAP, :], out2[...], in3[...]):
        total = total + part.astype(F32)
    out[0] = total[:, :BOX].astype(BF)
    out[1] = total[:, BOX:].astype(BF)


def call(kernel, outs, *args, scratch=(), flops=10**8, name=None, vmem=24, **kw):
    shapes = [jax.ShapeDtypeStruct(s, d) for s, d in outs]
    moved = sum(a.size * a.dtype.itemsize for a in args) + sum(s.size * s.dtype.itemsize for s in shapes)
    return pl.pallas_call(
        kernel,
        out_shape=shapes,
        scratch_shapes=list(scratch),
        compiler_params=pltpu.CompilerParams(vmem_limit_bytes=vmem * 2**20),
        cost_estimate=pl.CostEstimate(flops=flops, bytes_accessed=moved, transcendentals=0),
        name=name,
        **kw,
    )(*args)


def outward(value, steps):
    groups, count = lax.axis_size("box"), lax.axis_size("samp")
    pairs = []
    for b in range(groups):
        for i in range(count):
            j = (i + (steps if b % 2 == 0 else -steps)) % count
            pairs.append((b * count + i, b * count + j))
    return lax.ppermute(value, ("box", "samp"), pairs)


def across(value):
    groups = lax.axis_size("box")
    return lax.ppermute(value, "box", [(b, b ^ 1) for b in range(groups)])


def sideways(value, steps):
    groups = lax.axis_size("box")
    pairs = [(b, b + steps * (1 if b % 2 else -1)) for b in range(groups)]
    return lax.ppermute(value, "box", [(b, to) for b, to in pairs if 0 <= to < groups])


def on_device(
    currents, radiation, interp, anterp, weights, operators, pair_src, pair_op, pair_target
):
    rad = jnp.transpose(radiation, (0, 2, 3, 1)).reshape(2 * NS, P_SIZE)
    oper = operators.reshape(2 * NS, NOPS)
    weights = weights.reshape(1, NT)
    (edge,) = call(
        edge_kernel,
        [((TAIL + 16, CAP), BF)],
        *(pltpu.with_memory_space_constraint(a, pltpu.HBM) for a in (rad, anterp, weights)),
        scratch=[
            pltpu.VMEM((2 * NS, P_SIZE), BF),
            pltpu.VMEM((2 * WIDTH + 1, FD), F32),
            pltpu.VMEM((1, NT), F32),
            pltpu.SemaphoreType.DMA((EDGE_PARTS + 2,)),
        ],
        name="edge",
        in_specs=[HBM] * 3,
    )
    edge0 = outward(edge, 1)

    (field,) = call(field_kernel, [((NS, 2 * BOX), F32)], rad, currents, flops=10**9, name="field")
    inter, halo_mat, src_pick, oper_slot, slot_ids, oper_own, own_rows, own_mat = call(
        prepare_kernel,
        [
            ((NS, 2 * BOX), F32), ((2, 2, NS, EDGE), BF), ((BOX, SLOTS), BF),
            ((2 * NS, SLOTS), BF), ((16, SLOTS), BF), ((2 * NS, PAIR), BF), ((8, PAIR), jnp.int32),
            ((NS, 2 * NS), BF),
        ],
        field, interp, anterp, weights, pair_src, pair_op, pair_target, oper,
        flops=10**9,
        name="prepare",
    )
    edge0, inter, own_mat = lax.optimization_barrier((edge0, inter, own_mat))
    edge1 = across(edge0)
    (inter,) = call(
        first_edge_kernel, [((NS, 2 * BOX), F32)], inter, halo_mat, edge0, currents,
        flops=4 * 10**8, name="first_edge",
    )
    *buffers, rounded = call(
        send_kernel,
        [((BUF, CAP), BF)] * 4 + [((NS, 2 * BOX), BF)],
        inter, halo_mat, edge1, currents, src_pick, oper_slot, slot_ids,
        flops=4 * 10**8,
        name="send",
    )
    gots = [sideways(b, step) for b, step in zip(buffers, STEPS)]
    (own,) = call(
        own_kernel,
        [((NS, 2 * BOX), F32)],
        rounded, own_rows, oper_own,
        flops=10**9,
        name="own",
    )
    edge_mat, matrix = call(
        matrix_kernel,
        [((2 * EDGE, 2 * NS), BF), ((len(OUTWARD) * CAP, 2 * NS), BF)],
        rad, edge0, edge1, own_mat,
        flops=10**9,
        name="matrix",
    )
    blocks = lambda steps: (steps * CAP, 2 * BOX)
    leaving, stack = call(
        far_kernel,
        [(blocks(len(OUTWARD)), BF), ((2 * NS, 2 * BOX), BF)],
        own, matrix, *gots,
        flops=5 * 10**8,
        name="far",
    )
    from_inner = outward(leaving, 1)
    inward, keep = call(
        near_kernel,
        [(blocks(len(INWARD)), BF), (blocks(len(KEPT)), F32)],
        rad, edge0, edge1, own_mat, edge_mat, stack,
        scratch=[pltpu.VMEM(((len(INWARD) + len(KEPT)) * CAP, 2 * NS), BF)],
        flops=10**9,
        name="near",
    )
    from_outer = outward(inward, -1)
    (out2,) = call(relay_out_kernel, [(blocks(1), BF)], keep, from_inner, name="relay_out")
    from_inner2 = outward(out2, 2)
    (in3,) = call(relay_in_kernel, [(blocks(1), BF)], keep, from_inner, from_outer, name="relay_in")
    from_outer3 = outward(in3, -3)
    (out,) = call(
        sum_kernel,
        [((2, P_SIZE // RANKS, BOX), BF)],
        keep, from_inner, from_outer, from_inner2, from_outer3,
        name="total",
    )
    return out


def solution(mesh):
    return jax.shard_map(
        on_device,
        mesh=mesh,
        in_specs=(
            P(None, None, "box"),
            P(None, None, None, "samp"),
            P(None, "samp"),
            P(None, "samp"),
            P(),
            P(None, None, "samp", None),
            P("box"),
            P("box"),
            P("box"),
        ),
        out_specs=P(None, "samp", "box"),
        check_vma=False,
    )
```
